256 devices in a mesh: dp: 32 (over x, z_hi, core), feat: 8 (over y, z_lo).
Axes of the slice: x: 4, y: 4, z: 8 (z_hi: 4, z_lo: 2; z = z_hi * 2 + z_lo), core: 2. Of those that a mesh axis runs over, the one named last changes fastest.
Arguments:
- view_a: bfloat16 [4096, 8192], P('dp', 'feat'), as said below
- view_b: bfloat16 [4096, 8192], P('dp', 'feat'), as said below
Outputs:
- loss: float32 [], replicated
- grad_a: float32 [4096, 8192], P('dp', 'feat')
- grad_b: float32 [4096, 8192], P('dp', 'feat')
Inputs may be any that keep to these rules, and one draw needn't show every extreme that they name: `view_a`: real-valued projector outputs of order one to ten. `view_b`: real-valued projector outputs of order one to ten.
All inputs are finite; a program needn't handle non-finite values.
Results may differ from the reference program's by a relative error of at most 0.0065.
Values may be sent and summed in bfloat16 or wider, within the bound.
A program may use at most 64 MiB of HBM per device.

```python
import jax
import jax.numpy as jnp
from jax import lax

D = 8192
BATCH = 4096


def shared_base(key):
    first, second, third = jax.random.split(key, 3)
    own = jax.random.truncated_normal(first, -4.0, 4.0, (BATCH, D), jnp.float32)
    common = jax.random.truncated_normal(second, -4.0, 4.0, (BATCH, 256), jnp.float32)
    groups = jax.random.randint(third, (D,), 0, 256)
    return own + common[:, groups]


def finish(key, base, top):
    first, second, third = jax.random.split(key, 3)
    noise = jax.random.truncated_normal(first, -4.0, 4.0, (BATCH, D), jnp.float32)
    scale = jnp.exp(jax.random.uniform(second, (D,), jnp.float32, jnp.log(0.5), jnp.log(top)))
    offset = jax.random.uniform(third, (D,), jnp.float32, -1.0, 1.0)
    return ((base + 0.5 * noise) * scale + offset).astype(jnp.bfloat16)


def draw_view_a(key, part):
    base = shared_base(key)
    key = jax.random.fold_in(key, 11)
    return finish(key, base, 2.0)


def draw_view_b(key, part):
    base = shared_base(key)
    key = jax.random.fold_in(key, 23)
    return finish(key, base, 2.0)


def setup_inputs(seed: int = 0) -> dict:
    splits = jax.random.split(jax.random.key(seed), 3)
    view_a = draw_view_a(jax.random.fold_in(splits[2], 71), 0)
    view_b = draw_view_b(jax.random.fold_in(splits[2], 71), 0)
    return dict(view_a=view_a, view_b=view_b)


lam = 0.0051
eps = 1e-05

def normalize(view):
    values = view.astype(jnp.float32)
    mean = lax.optimization_barrier(jnp.sum(values, axis=0)) / BATCH
    centered = values - mean
    var = lax.optimization_barrier(jnp.sum(centered * centered, axis=0)) / BATCH
    rstd = lax.rsqrt(var + eps)
    return ((centered * rstd).astype(jnp.bfloat16), rstd)

def backnorm(upper, normed, rstd):
    first = lax.optimization_barrier(jnp.sum(upper, axis=0)) / BATCH
    second = lax.optimization_barrier(jnp.sum(upper * normed, axis=0)) / BATCH
    return rstd * (upper - first - normed * second)

def reference(view_a, view_b):
    norm_a, rstd_a = normalize(view_a)
    norm_b, rstd_b = normalize(view_b)
    full_a = norm_a.astype(jnp.float32)
    full_b = norm_b.astype(jnp.float32)
    corr = jnp.dot(full_a.T, full_b, precision=lax.Precision.HIGHEST) / BATCH
    diagonal = jnp.diagonal(corr)
    loss = lam * (jnp.sum(corr * corr) - jnp.sum(diagonal * diagonal)) + jnp.sum((1.0 - diagonal) ** 2)
    index = jnp.arange(D)
    grad_corr = (2.0 * lam * corr).at[index, index].set(2.0 * (diagonal - 1.0))
    grad_corr = grad_corr.astype(jnp.bfloat16).astype(jnp.float32)
    up_a = jnp.dot(full_b, grad_corr.T, precision=lax.Precision.HIGHEST)
    up_b = jnp.dot(full_a, grad_corr, precision=lax.Precision.HIGHEST)
    grad_a = backnorm(up_a, full_a, rstd_a)
    grad_b = backnorm(up_b, full_b, rstd_b)
    return (loss, grad_a, grad_b)
```

```python
import jax
import jax.numpy as jnp
from jax import lax
from jax.experimental import pallas as pl
from jax.experimental.pallas import tpu as pltpu
from jax.sharding import PartitionSpec as P

lam = 0.0051
eps = 1e-05
BATCH = 4096.0
WIDTH = 8192.0
MESH = pl.DeviceIdType.MESH
f32 = jnp.float32
bf16 = jnp.bfloat16

OFF = (0, 1, 3, 2)
BACK = {1: 2, 2: 1, 3: 3}

UNITS = ((0, 2, 0), (2, 2, 0), (2, 2, 1), (0, 2, 1), (2, 2, 2), (0, 2, 2), (2, 2, 3), (0, 2, 3))
NU = len(UNITS)


def kernel(
    va, vb, loss_ref, ga_ref, gb_ref,
    raw, nrm, oth, swap, st_x, st_z, st_mine, st_cross, st_out,
    gp, rsy, zs, rz, gf, us, u0, rs_same, rs_diff,
    mom, mx, mz, mc, ly, lz,
    core_s, core_r, gx_s, gx_r, gz_s, gz_r, sx_s, sx_r, sz_s, sz_r, oth_s, oth_r,
    y_s, y_r, z_s, z_r, az_s, az_r, ay_s, ay_r, us_s, us_r, ud_s, ud_r,
    mx_s, mx_r, mz_s, mz_r, m_s, m_r, ly_s, ly_r, lz_s, lz_r,
):
    dp = lax.axis_index("dp")
    ft = lax.axis_index("feat")
    x, zh, core = dp // 8, (dp // 2) % 4, dp % 2
    y, zl = ft // 2, ft % 2

    def dev(ax, az, ac, ay, al):
        return (ax * 8 + az * 2 + ac, ay * 2 + al)

    def xp(d):
        return dev((x + d) % 4, zh, core, y, zl)

    def xq(d):
        return dev((x + d) % 4, zh, 1 - core, y, zl)

    def zp(d):
        return dev(x, (zh + d) % 4, core, y, zl)

    def yp(d):
        return dev(x, zh, core, (y + d) % 4, zl)

    cp = dev(x, zh, 1 - core, y, zl)
    lp = dev(x, zh, core, y, 1 - zl)

    sends = []

    def send(src, dst, ss, rs, to):
        c = pltpu.make_async_remote_copy(
            src_ref=src, dst_ref=dst, send_sem=ss, recv_sem=rs, device_id=to, device_id_type=MESH
        )
        c.start()
        sends.append(c)
        return c

    barrier = pltpu.get_barrier_semaphore()
    peers = [cp, lp]
    for d in (1, 2, 3):
        peers += [xp(d), xq(d), zp(d), yp(d)]
    for p in peers:
        pl.semaphore_signal(barrier, inc=1, device_id=p, device_id_type=MESH)

    first = core == 0
    rows_c = pl.multiple_of(core * 128, 128)
    rows_o = pl.multiple_of((1 - core) * 128, 128)

    def split(i, _):
        r = pl.ds(pl.multiple_of(i * 32, 32), 32)
        a, b = va[r, :], vb[r, :]
        raw[0, pl.ds(pl.multiple_of(core * 128 + i * 32, 32), 32), :] = jnp.where(first, a, b)
        swap[r, :] = jnp.where(first, b, a)
        return 0

    lax.fori_loop(0, 4, split, 0)
    pl.semaphore_wait(barrier, len(peers))

    c = send(swap, raw.at[0, pl.ds(rows_c, 128), :], core_s.at[0], core_r.at[0], cp)
    c.wait_recv()

    lo, hi = pl.ds(0, 128), pl.ds(128, 128)

    def ring(base, ss, rs, to):
        def at(slot, rows):
            return raw.at[base + slot, rows, :]

        own_lo, own_hi = raw.at[0, lo, :], raw.at[0, hi, :]
        return (
            send(own_lo, at(2, lo), ss.at[0], rs.at[0], to(1)),
            send(own_hi, at(1, hi), ss.at[1], rs.at[1], to(3)),
            send(own_hi, at(2, hi), ss.at[2], rs.at[2], to(1)),
            send(own_lo, at(1, lo), ss.at[3], rs.at[3], to(3)),
        )

    def forward(base, ss, rs, to, near):
        near[0].wait_recv()
        a = send(raw.at[base + 2, lo, :], raw.at[base + 3, lo, :], ss.at[4], rs.at[4], to(1))
        near[1].wait_recv()
        b = send(raw.at[base + 1, hi, :], raw.at[base + 3, hi, :], ss.at[5], rs.at[5], to(3))
        return a, b

    gx = ring(0, gx_s, gx_r, xp)
    gz = ring(3, gz_s, gz_r, zp)

    def sums(i, acc):
        v = raw[0, pl.ds(pl.multiple_of(i * 32, 32), 32), :].astype(f32)
        return acc + jnp.sum(v.reshape(4, 8, 1024), axis=0)

    mean = jnp.sum(lax.fori_loop(0, 8, sums, jnp.zeros((8, 1024), f32)), axis=0, keepdims=True) / 256.0

    def squares(i, acc):
        v = raw[0, pl.ds(pl.multiple_of(i * 32, 32), 32), :].astype(f32) - mean
        return acc + jnp.sum((v * v).reshape(4, 8, 1024), axis=0)

    m2 = jnp.sum(lax.fori_loop(0, 8, squares, jnp.zeros((8, 1024), f32)), axis=0, keepdims=True)

    def combine(buf, count):
        means = [buf[k, 0:1, :] for k in range(4)]
        avg = (means[0] + means[1] + means[2] + means[3]) * 0.25
        total = buf[0, 1:2, :] + buf[1, 1:2, :] + buf[2, 1:2, :] + buf[3, 1:2, :]
        dev2 = sum((m - avg) * (m - avg) for m in means)
        return avg, total + count * dev2

    def spread(value_a, value_b, buf, me, ss, rs, to):
        buf[me, 0:1, :] = value_a
        buf[me, 1:2, :] = value_b
        cs = [send(buf.at[me], buf.at[me], ss.at[d - 1], rs.at[d - 1], to(d)) for d in (1, 2, 3)]
        for c in cs:
            c.wait_recv()

    spread(mean, m2, st_x, x, sx_s, sx_r, xp)
    mean, m2 = combine(st_x, 256.0)
    fx = forward(0, gx_s, gx_r, xp, gx)
    spread(mean, m2, st_z, zh, sz_s, sz_r, zp)
    mean, m2 = combine(st_z, 1024.0)
    rstd = lax.rsqrt(m2 / BATCH + eps)
    st_mine[0:1, :] = mean
    st_mine[1:2, :] = rstd
    cst = send(st_mine, st_cross, core_s.at[1], core_r.at[1], cp)

    def normalize(k):
        def step(i, _):
            r = pl.ds(pl.multiple_of(i * 32, 32), 32)
            v = raw[k, r, :].astype(f32)
            nrm[k, r, :] = ((v - st_mine[0:1, :]) * st_mine[1:2, :]).astype(bf16)
            return 0

        lax.fori_loop(0, 8, step, 0)
        return send(nrm.at[k], oth.at[k], oth_s.at[k], oth_r.at[k], cp)

    oc = {0: normalize(0)}
    gx[3].wait_recv()
    oc[1] = normalize(1)
    gx[2].wait_recv()
    oc[2] = normalize(2)
    fz = forward(3, gz_s, gz_r, zp, gz)

    ready = {"x3": False, 1: False, 2: False, 3: False}

    def need_row3():
        if not ready["x3"]:
            ready["x3"] = True
            fx[0].wait_recv()
            fx[1].wait_recv()
            oc[3] = normalize(3)

    def need_col(j):
        if j and not ready[j]:
            ready[j] = True
            if j == 1:
                gz[3].wait_recv()
            elif j == 2:
                gz[2].wait_recv()
            else:
                fz[0].wait_recv()
                fz[1].wait_recv()
            oc[3 + j] = normalize(3 + j)

    piece = pl.multiple_of(y * 64, 64)
    keep = pl.multiple_of(zl * 32, 32)
    give = pl.multiple_of((1 - zl) * 32, 32)
    nt = (((1,), (1,)), ((), ()))
    eye = (
        lax.broadcasted_iota(jnp.int32, (256, 256), 0) == lax.broadcasted_iota(jnp.int32, (256, 256), 1)
    )

    ry, zx, za, ay = {}, {}, {}, {}

    def stage0(u):
        i0, n, j = UNITS[u]
        if i0 + n > 3:
            need_row3()
        need_col(j)
        col = 0 if j == 0 else 3 + j
        for i in range(i0, i0 + n):
            g = lax.dot_general(nrm[i], nrm[col], nt, preferred_element_type=f32)
            if i == 0 and j == 0:
                g = jnp.where(eye, g - WIDTH / 8, g)
            gp[i, j] = g.astype(bf16)
        ry[u] = []
        for d in (2, 1, 3):
            r = pl.ds(pl.multiple_of(((y + d) % 4) * 64, 64), 64)
            ry[u].append(send(
                gp.at[pl.ds(i0, n), j, r, :], rsy.at[d - 1, pl.ds(i0, n), j],
                y_s.at[u, d - 1], y_r.at[u, d - 1], yp(d),
            ))

    def part(i, j, at):
        total = gp[i, j, pl.ds(pl.multiple_of(piece + at, 32), 32), :].astype(f32)
        for d in range(3):
            total = total + rsy[d, i, j, pl.ds(at, 32), :].astype(f32)
        return total

    def stage1(u):
        i0, n, j = UNITS[u]
        for c in ry[u]:
            c.wait_recv()
        for i in range(i0, i0 + n):
            zs[i, j] = part(i, j, give).astype(bf16)
        zx[u] = send(zs.at[pl.ds(i0, n), j], rz.at[pl.ds(i0, n), j], z_s.at[u], z_r.at[u], lp)

    def stage2(u):
        i0, n, j = UNITS[u]
        zx[u].wait_recv()
        r = pl.ds(pl.multiple_of(piece + keep, 32), 32)
        for i in range(i0, i0 + n):
            gf[i, j, r, :] = (part(i, j, keep) + rz[i, j].astype(f32)).astype(bf16)
        at = gf.at[pl.ds(i0, n), j, r, :]
        za[u] = send(at, at, az_s.at[u], az_r.at[u], lp)

    def stage3(u):
        i0, n, j = UNITS[u]
        za[u].wait_recv()
        at = gf.at[pl.ds(i0, n), j, pl.ds(piece, 64), :]
        ay[u] = [send(at, at, ay_s.at[u, d - 1], ay_r.at[u, d - 1], yp(d)) for d in (2, 1, 3)]

    for t in range(NU + 3):
        if t < NU:
            stage0(t)
        if 0 <= t - 1 < NU:
            stage1(t - 1)
        if 0 <= t - 2 < NU:
            stage2(t - 2)
        if 0 <= t - 3 < NU:
            stage3(t - 3)

    def own(i, acc):
        m = nrm[0, pl.ds(pl.multiple_of(core * 128 + i * 32, 32), 32), :].astype(f32)
        o = oth[0, pl.ds(pl.multiple_of(core * 128 + i * 32, 32), 32), :].astype(f32)
        return tuple(
            q + jnp.sum(v.reshape(4, 8, 1024), axis=0) for q, v in zip(acc, (m * o, m, o, m * m, o * o))
        )

    for k in range(7):
        oc[k].wait_recv()
    cst.wait_recv()
    ab, sm, so, mm, oo = (
        jnp.sum(v, axis=0, keepdims=True)
        for v in lax.fori_loop(0, 4, own, (jnp.zeros((8, 1024), f32),) * 5)
    )
    mom[0:1, :] = jnp.zeros((1, 1024), f32)
    mom[1:2, :] = jnp.zeros((1, 1024), f32)
    mom[2:3, :] = ab
    mom[3:4, :] = jnp.where(first, sm, so)
    mom[4:5, :] = jnp.where(first, so, sm)
    mom[5:6, :] = jnp.where(first, mm, oo)
    mom[6:7, :] = jnp.where(first, oo, mm)
    mom[7:8, :] = jnp.zeros((1, 1024), f32)

    def upper(i):
        def tile(t, _):
            cols = pl.ds(pl.multiple_of(t * 256, 256), 256)
            acc = jnp.dot(gf[i, 0], oth[0, :, cols], preferred_element_type=f32)
            for j in (1, 2, 3):
                acc = acc + jnp.dot(gf[i, j], oth[3 + j, :, cols], preferred_element_type=f32)
            us[i, :, cols] = acc.astype(bf16)
            if i == 0:
                u0[:, cols] = acc
            mom[0:1, cols] += jnp.sum(acc, axis=0, keepdims=True)
            mom[1:2, cols] += jnp.sum(acc * oth[i, :, cols].astype(f32), axis=0, keepdims=True)
            return 0

        lax.fori_loop(0, 4, tile, 0)

    same, diff = [], []
    seen = set()
    for i in (3, 2, 1, 0):
        for u in range(NU):
            i0, n, j = UNITS[u]
            if i0 <= i < i0 + n and u not in seen:
                seen.add(u)
                for c in ay[u]:
                    c.wait_recv()
        upper(i)
        if i:
            b = BACK[i]
            same.append(send(
                us.at[i, pl.ds(rows_c, 128), :], rs_same.at[b - 1],
                us_s.at[b - 1], us_r.at[b - 1], xp(OFF[i]),
            ))
            diff.append(send(
                us.at[i, pl.ds(rows_o, 128), :], rs_diff.at[b],
                ud_s.at[b], ud_r.at[b], xq(OFF[i]),
            ))
        else:
            diff.append(send(us.at[0, pl.ds(rows_o, 128), :], rs_diff.at[0], ud_s.at[0], ud_r.at[0], cp))

    def reduce(buf, me, ss, rs, to):
        buf[me] = mom[...]
        cs = [send(buf.at[me], buf.at[me], ss.at[d - 1], rs.at[d - 1], to(d)) for d in (1, 2, 3)]
        for c in cs:
            c.wait_recv()
        mom[...] = buf[0] + buf[1] + buf[2] + buf[3]

    reduce(mx, x, mx_s, mx_r, xp)
    reduce(mz, zh, mz_s, mz_r, zp)
    mc[core] = mom[...]
    send(mc.at[core], mc.at[core], m_s.at[0], m_r.at[0], cp).wait_recv()
    both = mc[0] + mc[1]
    ab, s_a, s_b, aa, bb = (both[k : k + 1, :] for k in range(2, 7))
    first_b, quad_b = mc[0, 0:1, :], mc[0, 1:2, :] + WIDTH * bb
    first_a, quad_a = mc[1, 0:1, :], mc[1, 1:2, :] + WIDTH * aa
    scale = 2.0 * lam / BATCH
    cii = ab / BATCH
    d = (2.0 * (cii - 1.0)).astype(bf16).astype(f32) - 2.0 * lam * cii
    one_a = (scale * (first_a + WIDTH * s_a) + d * s_b) / BATCH
    one_b = (scale * (first_b + WIDTH * s_b) + d * s_a) / BATCH
    two_a = (scale * quad_a + d * ab) / BATCH
    two_b = (scale * quad_b + d * ab) / BATCH

    terms = lam * (quad_b / (BATCH * BATCH) - cii * cii) + (1.0 - cii) * (1.0 - cii)
    ly[y] = jnp.broadcast_to(jnp.sum(terms, axis=1, keepdims=True), (8, 128))
    lc = [send(ly.at[y], ly.at[y], ly_s.at[k - 1], ly_r.at[k - 1], yp(k)) for k in (1, 2, 3)]

    one_m, two_m = jnp.where(first, one_a, one_b), jnp.where(first, two_a, two_b)
    one_c, two_c = jnp.where(first, one_b, one_a), jnp.where(first, two_b, two_a)
    for c in same + diff:
        c.wait_recv()
    for c in lc:
        c.wait_recv()
    lz[zl] = ly[0] + ly[1] + ly[2] + ly[3]
    lzc = send(lz.at[zl], lz.at[zl], lz_s.at[0], lz_r.at[0], lp)

    def finish(i, _):
        r = pl.ds(pl.multiple_of(i * 32, 32), 32)
        at = pl.ds(pl.multiple_of(core * 128 + i * 32, 32), 32)
        m, o = nrm[0, at, :].astype(f32), oth[0, at, :].astype(f32)
        up_c = u0[at, :]
        for k in range(3):
            up_c = up_c + rs_same[k, r, :].astype(f32)
        up_m = rs_diff[0, r, :].astype(f32)
        for k in range(1, 4):
            up_m = up_m + rs_diff[k, r, :].astype(f32)
        up_c = scale * (up_c + WIDTH * o) + d * m
        up_m = scale * (up_m + WIDTH * m) + d * o
        grad_m = st_mine[1:2, :] * (up_m - one_m - m * two_m)
        grad_c = st_cross[1:2, :] * (up_c - one_c - o * two_c)
        ga_ref[r, :] = jnp.where(first, grad_m, grad_c)
        gb_ref[r, :] = jnp.where(first, grad_c, grad_m)
        return 0

    lax.fori_loop(0, 4, finish, 0)
    lzc.wait_recv()
    loss_ref[...] = lz[0] + lz[1]
    for c in sends:
        c.wait_send()


def local(view_a, view_b):
    dma = pltpu.SemaphoreType.DMA
    vm = pltpu.VMEM
    sems = []
    for shape in (
        (2,), (6,), (6,), (3,), (3,), (7,), (NU, 3), (NU,), (NU,), (NU, 3), (3,), (4,),
        (3,), (3,), (1,), (3,), (1,),
    ):
        sems += [dma(shape), dma(shape)]
    vmem = pl.BlockSpec(memory_space=pltpu.VMEM)
    loss, grad_a, grad_b = pl.pallas_call(
        kernel,
        out_shape=(
            jax.ShapeDtypeStruct((8, 128), f32),
            jax.ShapeDtypeStruct((128, 1024), f32),
            jax.ShapeDtypeStruct((128, 1024), f32),
        ),
        in_specs=[vmem, vmem],
        out_specs=(vmem, vmem, vmem),
        scratch_shapes=[
            vm((7, 256, 1024), bf16), vm((7, 256, 1024), bf16), vm((7, 256, 1024), bf16),
            vm((128, 1024), bf16),
            vm((4, 8, 1024), f32), vm((4, 8, 1024), f32), vm((8, 1024), f32), vm((8, 1024), f32),
            vm((8, 1024), f32),
            vm((4, 4, 256, 256), bf16), vm((3, 4, 4, 64, 256), bf16),
            vm((4, 4, 32, 256), bf16), vm((4, 4, 32, 256), bf16),
            vm((4, 4, 256, 256), bf16),
            vm((4, 256, 1024), bf16), vm((256, 1024), f32),
            vm((3, 128, 1024), bf16), vm((4, 128, 1024), bf16),
            vm((8, 1024), f32), vm((4, 8, 1024), f32), vm((4, 8, 1024), f32), vm((2, 8, 1024), f32),
            vm((4, 8, 128), f32), vm((2, 8, 128), f32),
        ] + sems,
        compiler_params=pltpu.CompilerParams(
            collective_id=0, has_side_effects=True, vmem_limit_bytes=48 * 2**20
        ),
        name="twins",
    )(view_a, view_b)
    return loss[0, 0], grad_a, grad_b


def solution(mesh):
    placed = (P("dp", "feat"), P("dp", "feat"))
    return jax.shard_map(
        local,
        mesh=mesh,
        in_specs=placed,
        out_specs=(P(), P("dp", "feat"), P("dp", "feat")),
        check_vma=False,
    )
```

```python
import jax
import jax.numpy as jnp
from jax import lax
from jax.experimental import pallas as pl
from jax.experimental.pallas import tpu as pltpu
from jax.sharding import PartitionSpec as P

lam = 0.0051
eps = 1e-05
BATCH = 4096.0
WIDTH = 8192.0
MESH = pl.DeviceIdType.MESH
f32 = jnp.float32
bf16 = jnp.bfloat16

OFF = (0, 1, 3, 2)

UNITS = (
    (0, 0), (0, 1), (1, 0), (1, 1), (2, 1), (3, 0), (3, 1), (3, 2),
    (1, 2), (2, 2), (0, 2), (3, 3), (1, 3), (2, 3), (0, 3),
)
NU = len(UNITS)
RING = 11
ORDER = (
    (0, 0), (1, 0), (2, 0), (0, 1), (0, 2), (0, 3), (0, 4), (1, 1), (6, 1), (1, 2),
    (1, 3), (0, 5), (1, 4), (0, 6), (7, 0), (2, 1), (2, 2), (6, 2), (0, 7), (2, 3),
    (1, 5), (0, 8), (0, 9), (2, 4), (1, 6), (0, 10), (3, 0), (6, 3), (1, 7), (2, 5),
    (1, 8), (1, 9), (2, 6), (1, 10), (3, 1), (4, 0), (3, 2), (2, 7), (2, 8), (2, 9),
    (2, 10), (4, 1), (3, 3), (5, 0), (3, 4), (4, 2), (5, 1), (4, 3), (4, 4), (3, 5),
    (0, 11), (5, 2), (0, 12), (3, 6), (0, 13), (3, 7), (0, 14), (3, 8), (5, 3), (7, 1),
    (3, 9), (5, 4), (3, 10), (4, 5), (2, 11), (7, 2), (2, 12), (4, 6), (2, 13), (3, 11),
    (7, 3), (4, 7), (3, 12), (2, 14), (4, 8), (4, 9), (3, 13), (4, 10), (5, 5), (5, 6),
    (3, 14), (5, 11), (5, 7), (5, 12), (5, 8), (5, 9), (5, 13), (5, 10), (5, 14),
)
PARTS = 4


def kernel(
    va_hbm, vb_hbm, loss_ref, ga_ref, gb_ref,
    va, vb, raw, nrm, oth, swap, st_x, st_z, st_mine, st_cross,
    gp, rsy, ps, zs, rz, gf, us, u0, uf, relay, rs_same, rs_diff,
    mom, mc, mx, mz, own, ox, oz, oc2, ly, lz, lx, lsum,
    in_s, core_s, core_r, gx_s, gx_r, gz_s, gz_r, sx_s, sx_r, sz_s, sz_r, oth_s, oth_r,
    y_s, y_r, z_s, z_r, ay_s, ay_r, us_s, us_r, ud_s, ud_r, rl_s, rl_r,
    mx_s, mx_r, mz_s, mz_r, m_s, m_r, lx_s, lx_r, ox_s, ox_r, oz_s, oz_r, o_s, o_r, ly_s, ly_r, lz_s, lz_r,
):
    dp = lax.axis_index("dp")
    ft = lax.axis_index("feat")
    x, zh, core = dp // 8, (dp // 2) % 4, dp % 2
    y, zl = ft // 2, ft % 2

    def dev(ax, az, ac, ay, al):
        return (ax * 8 + az * 2 + ac, ay * 2 + al)

    def xp(d):
        return dev((x + d) % 4, zh, core, y, zl)

    def xq(d):
        return dev((x + d) % 4, zh, 1 - core, y, zl)

    def zp(d):
        return dev(x, (zh + d) % 4, core, y, zl)

    def yp(d):
        return dev(x, zh, core, (y + d) % 4, zl)

    def zq(d):
        return dev(x, (zh + d) % 4, 1 - core, y, zl)

    def yq(d):
        return dev(x, zh, core, (y + d) % 4, 1 - zl)

    cp = dev(x, zh, 1 - core, y, zl)
    lp = dev(x, zh, core, y, 1 - zl)

    sends = []

    def send(src, dst, ss, rs, to):
        c = pltpu.make_async_remote_copy(
            src_ref=src, dst_ref=dst, send_sem=ss, recv_sem=rs, device_id=to, device_id_type=MESH
        )
        c.start()
        sends.append(c)
        return c

    loads = [
        pltpu.make_async_copy(src, dst, in_s.at[k])
        for k, (src, dst) in enumerate(((va_hbm, va), (vb_hbm, vb)))
    ]
    for c in loads:
        c.start()
    barrier = pltpu.get_barrier_semaphore()
    peers = [cp, lp]
    for d in (1, 2, 3):
        peers += [xp(d), xq(d), zp(d), zq(d), yp(d), yq(d)]
    for p in peers:
        pl.semaphore_signal(barrier, inc=1, device_id=p, device_id_type=MESH)

    first = core == 0
    rows_c = pl.multiple_of(core * 128, 128)
    rows_o = pl.multiple_of((1 - core) * 128, 128)

    for c in loads:
        c.wait()

    def split(i, _):
        r = pl.ds(pl.multiple_of(i * 32, 32), 32)
        a, b = va[r, :], vb[r, :]
        raw[0, pl.ds(pl.multiple_of(core * 128 + i * 32, 32), 32), :] = jnp.where(first, a, b)
        swap[r, :] = jnp.where(first, b, a)
        return 0

    lax.fori_loop(0, 4, split, 0)
    pl.semaphore_wait(barrier, len(peers))

    c = send(swap, raw.at[0, pl.ds(rows_c, 128), :], core_s.at[0], core_r.at[0], cp)
    c.wait_recv()

    lo, hi = pl.ds(0, 128), pl.ds(128, 128)
    own_lo, own_hi = raw.at[0, lo, :], raw.at[0, hi, :]

    def ring(next_lo, next_hi, prev_lo, prev_hi, ss, rs, to):
        return (
            send(own_lo, prev_lo, ss.at[0], rs.at[0], to(1)),
            send(own_hi, next_hi, ss.at[1], rs.at[1], to(3)),
            send(own_hi, prev_hi, ss.at[2], rs.at[2], to(1)),
            send(own_lo, next_lo, ss.at[3], rs.at[3], to(3)),
        )

    def forward(prev_lo, next_hi, far, ss, rs, to, near):
        near[0].wait_recv()
        a = send(prev_lo, raw.at[far, lo, :], ss.at[4], rs.at[4], to(1))
        near[1].wait_recv()
        b = send(next_hi, raw.at[far, hi, :], ss.at[5], rs.at[5], to(3))
        return a, b

    def sums(i, acc):
        v = raw[0, pl.ds(pl.multiple_of(i * 32, 32), 32), :].astype(f32)
        return acc + jnp.sum(v.reshape(4, 8, 1024), axis=0)

    mean = jnp.sum(lax.fori_loop(0, 8, sums, jnp.zeros((8, 1024), f32)), axis=0, keepdims=True) / 256.0

    def squares(i, acc):
        v = raw[0, pl.ds(pl.multiple_of(i * 32, 32), 32), :].astype(f32) - mean
        return acc + jnp.sum((v * v).reshape(4, 8, 1024), axis=0)

    m2 = jnp.sum(lax.fori_loop(0, 8, squares, jnp.zeros((8, 1024), f32)), axis=0, keepdims=True)

    def combine(buf, count):
        means = [buf[k, 0:1, :] for k in range(4)]
        avg = (means[0] + means[1] + means[2] + means[3]) * 0.25
        total = buf[0, 1:2, :] + buf[1, 1:2, :] + buf[2, 1:2, :] + buf[3, 1:2, :]
        dev2 = sum((m - avg) * (m - avg) for m in means)
        return avg, total + count * dev2

    def spread(value_a, value_b, buf, me, ss, rs, to):
        buf[me, 0:1, :] = value_a
        buf[me, 1:2, :] = value_b
        return [send(buf.at[me], buf.at[me], ss.at[d - 1], rs.at[d - 1], to(d)) for d in (1, 2, 3)]

    sz = spread(mean, m2, st_z, zh, sz_s, sz_r, zp)
    gz = ring(
        raw.at[5, lo, :], raw.at[4, lo, :], raw.at[4, hi, :], raw.at[5, hi, :], gz_s, gz_r, zp
    )
    for c in sz:
        c.wait_recv()
    mean, m2 = combine(st_z, 256.0)
    sx = spread(mean, m2, st_x, x, sx_s, sx_r, xp)
    gx = ring(
        raw.at[1, lo, :], raw.at[1, hi, :], raw.at[2, lo, :], raw.at[2, hi, :], gx_s, gx_r, xp
    )
    for c in sx:
        c.wait_recv()
    mean, m2 = combine(st_x, 1024.0)
    rstd = lax.rsqrt(m2 / BATCH + eps)
    st_mine[0:1, :] = mean
    st_mine[1:2, :] = rstd
    cst = send(st_mine, st_cross, core_s.at[1], core_r.at[1], cp)

    def normalize(k):
        def step(i, _):
            r = pl.ds(pl.multiple_of(i * 32, 32), 32)
            v = raw[k, r, :].astype(f32)
            nrm[k, r, :] = ((v - st_mine[0:1, :]) * st_mine[1:2, :]).astype(bf16)
            return 0

        lax.fori_loop(0, 8, step, 0)
        return send(nrm.at[k], oth.at[k], oth_s.at[k], oth_r.at[k], cp)

    oc = {0: normalize(0)}
    far = {}

    def forward_x():
        far["x"] = forward(raw.at[2, lo, :], raw.at[1, hi, :], 3, gx_s, gx_r, xp, gx)

    def forward_z(k):
        if k >= PARTS:
            return
        n = 128 // PARTS
        for e, (half, to) in enumerate(((1, 1), (0, 3))):
            if k == 0:
                gz[e].wait_recv()
            src = raw.at[4, pl.ds(half * 128 + k * n, n), :]
            dst = raw.at[6, pl.ds((1 - half) * 128 + k * n, n), :]
            at = 4 + 2 * k + e
            far.setdefault("z", []).append(send(src, dst, gz_s.at[at], gz_r.at[at], zp(to)))

    arrive = {
        1: lambda: gx[3].wait_recv(),
        2: lambda: gx[2].wait_recv(),
        3: lambda: [c.wait_recv() for c in far["x"]],
        4: lambda: [forward_x(), forward_z(0)],
        5: lambda: [gz[2].wait_recv(), gz[3].wait_recv()],
        6: lambda: [c.wait_recv() for c in far["z"]],
    }

    def need(k):
        if k not in oc:
            arrive[k]()
            oc[k] = normalize(k)

    piece = pl.multiple_of(y * 64, 64)
    nt = (((1,), (1,)), ((), ()))
    eye = (
        lax.broadcasted_iota(jnp.int32, (256, 256), 0) == lax.broadcasted_iota(jnp.int32, (256, 256), 1)
    )

    ry, zx, ay = {}, {}, {}
    mine = pl.ds(piece, 64)

    def rows_of(d, at=0, n=64):
        return pl.ds(pl.multiple_of(((y + d) % 4) * 64 + at, 32), n)

    def stage0(u):
        i, j = UNITS[u]
        col = 3 + j if j else 0
        need(col)
        need(i)
        g = lax.dot_general(nrm[i], nrm[col], nt, preferred_element_type=f32)
        if i == 0 and j == 0:
            g = jnp.where(eye, g - WIDTH / 8, g)
        gp[i, j] = g.astype(bf16)
        if u < RING:
            ry[u] = [
                send(gp.at[i, j, rows_of(2, 0, 32), :], rsy.at[2, i, j, pl.ds(0, 32), :],
                     y_s.at[u, 0], y_r.at[u, 0], yp(1)),
                send(gp.at[i, j, rows_of(2, 32, 32), :], rsy.at[2, i, j, pl.ds(32, 32), :],
                     y_s.at[u, 1], y_r.at[u, 1], yp(3)),
            ]
        else:
            ry[u] = [
                send(gp.at[i, j, rows_of(d), :], rsy.at[d - 1, i, j], y_s.at[u, d - 1], y_r.at[u, d - 1], yp(d))
                for d in (2, 1, 3)
            ]

    def relay_y(u):
        i, j = UNITS[u]
        for c in ry[u]:
            c.wait_recv()
        up = rsy[2, i, j, 0:32, :].astype(f32) + gp[i, j, rows_of(1, 0, 32), :].astype(f32)
        ps[0, i, j, 0:32, :] = up.astype(bf16)
        ps[0, i, j, 32:64, :] = gp[i, j, rows_of(1, 32, 32), :]
        down = rsy[2, i, j, 32:64, :].astype(f32) + gp[i, j, rows_of(3, 32, 32), :].astype(f32)
        ps[1, i, j, 0:32, :] = gp[i, j, rows_of(3, 0, 32), :]
        ps[1, i, j, 32:64, :] = down.astype(bf16)
        ry[u] = [
            send(ps.at[k, i, j], rsy.at[k, i, j], y_s.at[u, 2 + k], y_r.at[u, 2 + k], yp(1 + 2 * k))
            for k in range(2)
        ]

    def stage1(u):
        i, j = UNITS[u]
        for c in ry[u]:
            c.wait_recv()
        total = gp[i, j, mine, :].astype(f32)
        for k in range(2 if u < RING else 3):
            total = total + rsy[k, i, j].astype(f32)
        zs[i, j] = total.astype(bf16)
        zx[u] = send(zs.at[i, j], rz.at[i, j], z_s.at[u], z_r.at[u], lp)

    def stage2(u):
        i, j = UNITS[u]
        zx[u].wait_recv()
        gf[i, j, mine, :] = (zs[i, j].astype(f32) + rz[i, j].astype(f32)).astype(bf16)
        at = gf.at[i, j, mine, :]
        ay[u] = [
            send(at, at, ay_s.at[u, d - 1], ay_r.at[u, d - 1], yp(d)) for d in ((1, 3) if u < RING else (2, 1, 3))
        ]

    def pass_y(u):
        i, j = UNITS[u]
        for c in ay[u]:
            c.wait_recv()
        a = gf.at[i, j, rows_of(3, 0, 32), :]
        b = gf.at[i, j, rows_of(1, 32, 32), :]
        ay[u] = [
            send(a, a, ay_s.at[u, 1], ay_r.at[u, 1], yp(1)),
            send(b, b, ay_s.at[u, 3], ay_r.at[u, 3], yp(3)),
        ]

    def step_own(i, acc):
        at = pl.ds(pl.multiple_of(core * 128 + i * 32, 32), 32)
        m, o = nrm[0, at, :].astype(f32), oth[0, at, :].astype(f32)
        return tuple(
            q + jnp.sum(v.reshape(4, 8, 1024), axis=0) for q, v in zip(acc, (m * o, m, o, m * m, o * o))
        )

    def hop(src, buf, me, ss, rs, to):
        buf[me] = src[...]
        return [send(buf.at[me], buf.at[me], ss.at[d - 1], rs.at[d - 1], to(d)) for d in (1, 2, 3)]

    def swap_cores(src, buf, ss, rs):
        buf[core] = src[...]
        return [send(buf.at[core], buf.at[core], ss.at[0], rs.at[0], cp)]

    def gathered(dst, buf, n, cs):
        for c in cs:
            c.wait_recv()
        total = buf[0]
        for k in range(1, n):
            total = total + buf[k]
        dst[...] = total

    pend = {}

    def own0():
        oc[0].wait_recv()
        ab, sm, so, mm, oo = (
            jnp.sum(v, axis=0, keepdims=True)
            for v in lax.fori_loop(0, 4, step_own, (jnp.zeros((8, 1024), f32),) * 5)
        )
        rows = (
            ab, jnp.where(first, sm, so), jnp.where(first, so, sm),
            jnp.where(first, mm, oo), jnp.where(first, oo, mm),
        )
        for k, v in enumerate(rows):
            own[k : k + 1, :] = v
        own[5:8, :] = jnp.zeros((3, 1024), f32)
        pend["own"] = hop(own, oz, zh, oz_s, oz_r, zp)

    def own1():
        gathered(own, oz, 4, pend["own"])
        pend["own"] = swap_cores(own, oc2, o_s, o_r)

    def own2():
        gathered(own, oc2, 2, pend["own"])
        pend["own"] = hop(own, ox, x, ox_s, ox_r, xp)

    def own3():
        gathered(own, ox, 4, pend["own"])

    mom[...] = jnp.zeros((2, 2, 1024), f32)
    tn = (((0,), (0,)), ((), ()))

    def upper(i):
        blocks = [j for j in range(4) if (i, j) in UNITS]

        def tile(t, _):
            cols = pl.ds(pl.multiple_of(t * 256, 256), 256)
            acc = jnp.zeros((256, 256), f32)
            for j in blocks:
                acc = acc + jnp.dot(gf[i, j], oth[3 + j if j else 0, :, cols], preferred_element_type=f32)
            if i == 0:
                acc = acc + lax.dot_general(gf[1, 0], oth[1, :, cols], tn, preferred_element_type=f32)
                u0[:, cols] = acc
            elif i < 3:
                uf[i - 1, :, cols] = acc
            us[i, :, cols] = acc.astype(bf16)
            one = jnp.sum(acc, axis=0, keepdims=True)
            two = jnp.sum(acc * oth[i, :, cols].astype(f32), axis=0, keepdims=True)
            mom[core, 0:1, cols] += one
            mom[core, 1:2, cols] += two
            return 0

        lax.fori_loop(0, 4, tile, 0)

    same, diff = [], []
    got = set()

    def stage3(u):
        for c in ay[u]:
            c.wait_recv()
        got.add(UNITS[u])
        i = UNITS[u][0]
        if not all(v in got for v in UNITS if v[0] == i):
            return
        for j in range(4):
            k = 3 + j if j else 0
            if k in oc and k not in ready:
                ready.add(k)
                if k:
                    oc[k].wait_recv()
        for k in (i, 1):
            if k not in ready:
                ready.add(k)
                oc[k].wait_recv()
        upper(i)
        rows_same, rows_diff = pl.ds(rows_c, 128), pl.ds(rows_o, 128)
        if i == 3:
            relays.append(send(us.at[3, rows_same, :], relay.at[0], rl_s.at[0], rl_r.at[0], xp(1)))
            relays.append(send(us.at[3, rows_diff, :], relay.at[1], rl_s.at[1], rl_r.at[1], xp(3)))
        elif i == 1:
            diff.append(send(us.at[1, rows_diff, :], rs_diff.at[1], ud_s.at[1], ud_r.at[1], xq(1)))
        elif i == 2:
            same.append(send(us.at[2, rows_same, :], rs_same.at[1], us_s.at[1], us_r.at[1], xp(3)))
        else:
            diff.append(send(us.at[0, rows_diff, :], rs_diff.at[0], ud_s.at[0], ud_r.at[0], cp))

    def pass_x(k):
        start = rows_o if k else rows_c
        relays[k].wait_recv()

        def add(t, _):
            r = pl.ds(pl.multiple_of(t * 32, 32), 32)
            at = pl.ds(pl.multiple_of(start + t * 32, 32), 32)
            us[k + 1, at, :] = (uf[k, at, :] + relay[k, r, :].astype(f32)).astype(bf16)
            return 0

        lax.fori_loop(0, 4, add, 0)
        src = us.at[k + 1, pl.ds(start, 128), :]
        if k == 0:
            same.append(send(src, rs_same.at[0], us_s.at[0], us_r.at[0], xp(1)))
        else:
            diff.append(send(src, rs_diff.at[2], ud_s.at[2], ud_r.at[2], xq(3)))

    relays = []
    ready = {0}
    stages = (stage0, relay_y, stage1, stage2, pass_y, stage3)
    owns = (own0, own1, own2, own3)
    for stage, u in ORDER:
        if stage < 6:
            stages[stage](u)
        elif stage == 6:
            forward_z(u)
        else:
            owns[u]()

    mc[core] = mom[core]
    mc_wait = send(mc.at[core], mc.at[core], m_s.at[0], m_r.at[0], cp)
    cst.wait_recv()
    ab, s_a, s_b, aa, bb = (own[k : k + 1, :] for k in range(5))
    scale = 2.0 * lam / BATCH
    cii = ab / BATCH
    d = (2.0 * (cii - 1.0)).astype(bf16).astype(f32) - 2.0 * lam * cii

    norms = WIDTH * (aa + bb) / (BATCH * BATCH)
    pairs = mom[core, 1:2, :] / (BATCH * BATCH)
    terms = 0.5 * lam * pairs + (
        lam * (0.5 * norms - cii * cii) + (1.0 - cii) * (1.0 - cii)
    ) / 32.0
    ly[ft] = jnp.broadcast_to(jnp.sum(terms, axis=1, keepdims=True), (8, 128))
    ly_wait = []
    for k in (1, 2, 3):
        ly_wait.append(send(ly.at[ft], ly.at[ft], ly_s.at[k], ly_r.at[k], yp(k)))
        ly_wait.append(send(ly.at[ft], ly.at[ft], ly_s.at[k + 3], ly_r.at[k + 3], yq(k)))
    ly_wait.append(send(ly.at[ft], ly.at[ft], ly_s.at[0], ly_r.at[0], lp))
    pass_x(0)
    pass_x(1)
    mc_wait.wait_recv()
    mz_wait = hop(mc, mz, zh, mz_s, mz_r, zp)
    lme = zh * 2 + core
    gathered(lz.at[lme], ly, 8, ly_wait)
    lz_wait = []
    for k in (1, 2, 3):
        lz_wait.append(send(lz.at[lme], lz.at[lme], lz_s.at[k], lz_r.at[k], zp(k)))
        lz_wait.append(send(lz.at[lme], lz.at[lme], lz_s.at[k + 3], lz_r.at[k + 3], zq(k)))
    lz_wait.append(send(lz.at[lme], lz.at[lme], lz_s.at[0], lz_r.at[0], cp))
    gathered(mom, mz, 4, mz_wait)
    mx_wait = hop(mom, mx, x, mx_s, mx_r, xp)
    gathered(lsum, lz, 8, lz_wait)
    lx_wait = hop(lsum, lx, x, lx_s, lx_r, xp)
    gathered(mom, mx, 4, mx_wait)

    first_b, quad_b, first_a, quad_a = (mom[c, k : k + 1, :] for c in range(2) for k in range(2))
    one_a = (scale * (first_a + WIDTH * s_a) + d * s_b) / BATCH
    one_b = (scale * (first_b + WIDTH * s_b) + d * s_a) / BATCH
    two_a = (scale * (quad_a + WIDTH * aa) + d * ab) / BATCH
    two_b = (scale * (quad_b + WIDTH * bb) + d * ab) / BATCH
    one_m, two_m = jnp.where(first, one_a, one_b), jnp.where(first, two_a, two_b)
    one_c, two_c = jnp.where(first, one_b, one_a), jnp.where(first, two_b, two_a)
    for c in same + diff:
        c.wait_recv()

    def finish(i, _):
        r = pl.ds(pl.multiple_of(i * 32, 32), 32)
        at = pl.ds(pl.multiple_of(core * 128 + i * 32, 32), 32)
        m, o = nrm[0, at, :].astype(f32), oth[0, at, :].astype(f32)
        up_c = u0[at, :] + rs_same[0, r, :].astype(f32) + rs_same[1, r, :].astype(f32)
        up_m = rs_diff[0, r, :].astype(f32) + rs_diff[1, r, :].astype(f32) + rs_diff[2, r, :].astype(f32)
        up_c = scale * (up_c + WIDTH * o) + d * m
        up_m = scale * (up_m + WIDTH * m) + d * o
        grad_m = st_mine[1:2, :] * (up_m - one_m - m * two_m)
        grad_c = st_cross[1:2, :] * (up_c - one_c - o * two_c)
        ga_ref[r, :] = jnp.where(first, grad_m, grad_c)
        gb_ref[r, :] = jnp.where(first, grad_c, grad_m)
        return 0

    lax.fori_loop(0, 4, finish, 0)
    gathered(lsum, lx, 4, lx_wait)
    loss_ref[...] = lsum[0:1, 0:1]
    for c in sends:
        c.wait_send()


def local(view_a, view_b):
    dma = pltpu.SemaphoreType.DMA
    vm = pltpu.VMEM
    sems = [dma((2,))]
    for shape in (
        (2,), (6,), (4 + 2 * PARTS,), (3,), (3,), (7,), (NU, 4), (NU,), (NU, 4), (2,), (3,), (2,),
        (3,), (3,), (1,), (3,), (3,), (3,), (1,), (7,), (7,),
    ):
        sems += [dma(shape), dma(shape)]
    vmem = pl.BlockSpec(memory_space=pltpu.VMEM)
    loss, grad_a, grad_b = pl.pallas_call(
        kernel,
        out_shape=(
            jax.ShapeDtypeStruct((1, 1), f32),
            jax.ShapeDtypeStruct((128, 1024), f32),
            jax.ShapeDtypeStruct((128, 1024), f32),
        ),
        in_specs=[pl.BlockSpec(memory_space=pl.ANY)] * 2,
        out_specs=(vmem, vmem, vmem),
        scratch_shapes=[
            vm((128, 1024), bf16), vm((128, 1024), bf16),
            vm((7, 256, 1024), bf16), vm((7, 256, 1024), bf16), vm((7, 256, 1024), bf16),
            vm((128, 1024), bf16),
            vm((4, 2, 1024), f32), vm((4, 2, 1024), f32), vm((8, 1024), f32), vm((8, 1024), f32),
            vm((4, 4, 256, 256), bf16), vm((3, 4, 4, 64, 256), bf16), vm((2, 4, 4, 64, 256), bf16),
            vm((4, 4, 64, 256), bf16), vm((4, 4, 64, 256), bf16),
            vm((4, 4, 256, 256), bf16),
            vm((4, 256, 1024), bf16), vm((256, 1024), f32),
            vm((2, 256, 1024), f32), vm((2, 128, 1024), bf16),
            vm((2, 128, 1024), bf16), vm((3, 128, 1024), bf16),
            vm((2, 2, 1024), f32), vm((2, 2, 1024), f32), vm((4, 2, 2, 1024), f32), vm((4, 2, 2, 1024), f32),
            vm((8, 1024), f32), vm((4, 8, 1024), f32), vm((4, 8, 1024), f32), vm((2, 8, 1024), f32),
            vm((8, 8, 128), f32), vm((8, 8, 128), f32), vm((4, 8, 128), f32), vm((8, 128), f32),
        ] + sems,
        compiler_params=pltpu.CompilerParams(
            collective_id=0, has_side_effects=True, vmem_limit_bytes=48 * 2**20
        ),
        name="twins",
    )(view_a, view_b)
    return loss[0, 0], grad_a, grad_b


def solution(mesh):
    placed = (P("dp", "feat"), P("dp", "feat"))
    return jax.shard_map(
        local,
        mesh=mesh,
        in_specs=placed,
        out_specs=(P(), P("dp", "feat"), P("dp", "feat")),
        check_vma=False,
    )
```

```python
import jax
import jax.numpy as jnp
from jax import lax
from jax.experimental import pallas as pl
from jax.experimental.pallas import tpu as pltpu
from jax.sharding import PartitionSpec as P

lam = 0.0051
eps = 1e-05
BATCH = 4096.0
WIDTH = 8192.0
MESH = pl.DeviceIdType.MESH
f32 = jnp.float32
bf16 = jnp.bfloat16

OFF = (0, 1, 3, 2)

UNITS = (
    (0, 0), (0, 1), (1, 0), (1, 1), (2, 1), (3, 0), (3, 1), (3, 2),
    (1, 2), (2, 2), (0, 2), (1, 3), (2, 3), (0, 3), (3, 3),
)
NU = len(UNITS)
RING = 11
ORDER = (
    (0, 0), (1, 0), (2, 0), (0, 1), (0, 2), (0, 3), (0, 4), (6, 1), (1, 1), (1, 2),
    (6, 2), (1, 3), (0, 5), (1, 4), (0, 6), (7, 0), (2, 1), (6, 3), (2, 2), (0, 7),
    (2, 3), (1, 5), (6, 4), (2, 4), (8, 0), (1, 6), (3, 0), (0, 8), (6, 5), (8, 1),
    (1, 7), (7, 1), (2, 5), (2, 6), (8, 2), (3, 1), (0, 9), (6, 6), (4, 0), (1, 8),
    (2, 7), (8, 3), (3, 2), (0, 10), (6, 7), (3, 3), (4, 1), (1, 9), (5, 0), (8, 4),
    (2, 8), (3, 4), (4, 2), (1, 10), (4, 3), (8, 5), (5, 1), (3, 5), (2, 9), (3, 6),
    (4, 4), (5, 2), (2, 10), (8, 6), (5, 3), (3, 7), (4, 5), (4, 6), (5, 4), (8, 7),
    (7, 2), (0, 11), (3, 8), (0, 12), (0, 13), (3, 9), (4, 7), (3, 10), (5, 5), (5, 6),
    (2, 11), (0, 14), (4, 8), (2, 12), (2, 13), (3, 11), (4, 9), (5, 7), (4, 10), (3, 12),
    (2, 14), (5, 8), (3, 13), (5, 11), (5, 9), (5, 10), (3, 14), (5, 12), (5, 13), (7, 3),
    (7, 4), (10, 0), (10, 1), (5, 14),
)
POOL = 48
PARTS = 8


def kernel(
    va_hbm, vb_hbm, loss_ref, ga_ref, gb_ref,
    va, vb, raw, nrm, oth, swap, st_x, st_z, st_mine, st_cross,
    gp, rsy, ps, zs, rz, gf, us, u0, uf, relay, rs_same, rs_diff,
    mom, mx, mz, pc, own, ox, oz, oc2, ly, lz, lx, lsum,
    in_s, pool_s, core_s, gx_s, gz_s, oth_s, us_s, ud_s, rl_s,
    core_r, gx_r, gz_r, oth_r, us_r, ud_r, rl_r, y_r, z_r, ay_r,
    sx_r, sz_r, mx_r, mz_r, pc_r, ox_r, oz_r, o_r, ly_r, lz_r, lx_r,
):
    dp = lax.axis_index("dp")
    ft = lax.axis_index("feat")
    x, zh, core = dp // 8, (dp // 2) % 4, dp % 2
    y, zl = ft // 2, ft % 2

    def dev(ax, az, ac, ay, al):
        return (ax * 8 + az * 2 + ac, ay * 2 + al)

    def xp(d):
        return dev((x + d) % 4, zh, core, y, zl)

    def xq(d):
        return dev((x + d) % 4, zh, 1 - core, y, zl)

    def zp(d):
        return dev(x, (zh + d) % 4, core, y, zl)

    def yp(d):
        return dev(x, zh, core, (y + d) % 4, zl)

    def zq(d):
        return dev(x, (zh + d) % 4, 1 - core, y, zl)

    def yq(d):
        return dev(x, zh, core, (y + d) % 4, 1 - zl)

    cp = dev(x, zh, 1 - core, y, zl)
    lp = dev(x, zh, core, y, 1 - zl)

    sends, busy, turn = [], {}, [0]

    def send(src, dst, ss, rs, to):
        slot = None
        if ss is None:
            slot = turn[0] % POOL
            turn[0] += 1
            if slot in busy:
                busy[slot].wait_send()
            ss = pool_s.at[slot]
        c = pltpu.make_async_remote_copy(
            src_ref=src, dst_ref=dst, send_sem=ss, recv_sem=rs, device_id=to, device_id_type=MESH
        )
        c.start()
        if slot is None:
            sends.append(c)
        else:
            busy[slot] = c
        return c

    class Group:
        def __init__(self, buf, rs):
            self.buf, self.rs = buf, rs

        def wait_recv(self):
            pltpu.make_async_remote_copy(
                src_ref=self.buf, dst_ref=self.buf, send_sem=pool_s.at[0], recv_sem=self.rs,
                device_id=cp, device_id_type=MESH,
            ).wait_recv()

    loads = [
        pltpu.make_async_copy(src, dst, in_s.at[k])
        for k, (src, dst) in enumerate(((va_hbm, va), (vb_hbm, vb)))
    ]
    for c in loads:
        c.start()
    barrier = pltpu.get_barrier_semaphore()
    peers = [cp, lp]
    for d in (1, 2, 3):
        peers += [xp(d), xq(d), zp(d), zq(d), yp(d), yq(d)]
    for p in peers:
        pl.semaphore_signal(barrier, inc=1, device_id=p, device_id_type=MESH)

    first = core == 0
    rows_c = pl.multiple_of(core * 128, 128)
    rows_o = pl.multiple_of((1 - core) * 128, 128)

    for c in loads:
        c.wait()

    def split(i, _):
        r = pl.ds(pl.multiple_of(i * 32, 32), 32)
        a, b = va[r, :], vb[r, :]
        raw[0, pl.ds(pl.multiple_of(core * 128 + i * 32, 32), 32), :] = jnp.where(first, a, b)
        swap[r, :] = jnp.where(first, b, a)
        return 0

    lax.fori_loop(0, 4, split, 0)
    pl.semaphore_wait(barrier, len(peers))

    c = send(swap, raw.at[0, pl.ds(rows_c, 128), :], core_s.at[0], core_r.at[0], cp)
    c.wait_recv()

    lo, hi = pl.ds(0, 128), pl.ds(128, 128)
    own_lo, own_hi = raw.at[0, lo, :], raw.at[0, hi, :]

    def ring(next_lo, next_hi, prev_lo, prev_hi, ss, rs, to):
        return (
            send(own_lo, prev_lo, ss.at[0], rs.at[0], to(1)),
            send(own_hi, next_hi, ss.at[1], rs.at[1], to(3)),
            send(own_hi, prev_hi, ss.at[2], rs.at[2], to(1)),
            send(own_lo, next_lo, ss.at[3], rs.at[3], to(3)),
        )

    def forward(prev_lo, next_hi, far, ss, rs, to, near):
        near[0].wait_recv()
        send(prev_lo, raw.at[far, lo, :], ss.at[4], rs.at[4], to(1))
        near[1].wait_recv()
        send(next_hi, raw.at[far, hi, :], ss.at[5], rs.at[4], to(3))
        return [Group(raw.at[far], rs.at[4])]

    def sums(i, acc):
        v = raw[0, pl.ds(pl.multiple_of(i * 32, 32), 32), :].astype(f32)
        return acc + jnp.sum(v.reshape(4, 8, 1024), axis=0)

    mean = jnp.sum(lax.fori_loop(0, 8, sums, jnp.zeros((8, 1024), f32)), axis=0, keepdims=True) / 256.0

    def squares(i, acc):
        v = raw[0, pl.ds(pl.multiple_of(i * 32, 32), 32), :].astype(f32) - mean
        return acc + jnp.sum((v * v).reshape(4, 8, 1024), axis=0)

    m2 = jnp.sum(lax.fori_loop(0, 8, squares, jnp.zeros((8, 1024), f32)), axis=0, keepdims=True)

    def combine(buf, count):
        means = [buf[k, 0:1, :] for k in range(4)]
        avg = (means[0] + means[1] + means[2] + means[3]) * 0.25
        total = buf[0, 1:2, :] + buf[1, 1:2, :] + buf[2, 1:2, :] + buf[3, 1:2, :]
        dev2 = sum((m - avg) * (m - avg) for m in means)
        return avg, total + count * dev2

    def spread(value_a, value_b, buf, me, rs, to):
        buf[me, 0:1, :] = value_a
        buf[me, 1:2, :] = value_b
        for d in (1, 2, 3):
            send(buf.at[me], buf.at[me], None, rs.at[0], to(d))
        return [Group(buf.at[0:3], rs.at[0])]

    sz = spread(mean, m2, st_z, zh, sz_r, zp)
    gz = ring(
        raw.at[5, lo, :], raw.at[4, lo, :], raw.at[4, hi, :], raw.at[5, hi, :], gz_s, gz_r, zp
    )
    for c in sz:
        c.wait_recv()
    mean, m2 = combine(st_z, 256.0)
    sx = spread(mean, m2, st_x, x, sx_r, xp)
    gx = ring(
        raw.at[1, lo, :], raw.at[1, hi, :], raw.at[2, lo, :], raw.at[2, hi, :], gx_s, gx_r, xp
    )
    for c in sx:
        c.wait_recv()
    mean, m2 = combine(st_x, 1024.0)
    rstd = lax.rsqrt(m2 / BATCH + eps)
    st_mine[0:1, :] = mean
    st_mine[1:2, :] = rstd
    cst = send(st_mine, st_cross, core_s.at[1], core_r.at[1], cp)

    def normalize(k):
        def step(i, _):
            r = pl.ds(pl.multiple_of(i * 32, 32), 32)
            v = raw[k, r, :].astype(f32)
            nrm[k, r, :] = ((v - st_mine[0:1, :]) * st_mine[1:2, :]).astype(bf16)
            return 0

        lax.fori_loop(0, 8, step, 0)
        return send(nrm.at[k], oth.at[k], oth_s.at[k], oth_r.at[k], cp)

    oc = {0: normalize(0)}
    far = {}

    def forward_x():
        far["x"] = forward(raw.at[2, lo, :], raw.at[1, hi, :], 3, gx_s, gx_r, xp, gx)

    def forward_z(k):
        if k >= PARTS:
            return
        n = 128 // PARTS
        for e, (half, to) in enumerate(((1, 1), (0, 3))):
            if k == 0:
                gz[e].wait_recv()
            src = raw.at[4, pl.ds(half * 128 + k * n, n), :]
            dst = raw.at[6, pl.ds((1 - half) * 128 + k * n, n), :]
            send(src, dst, gz_s.at[4 + 2 * k + e], gz_r.at[4 + k], zp(to))

    def pass_far(k):
        n = 128 // PARTS
        Group(raw.at[6, pl.ds(0, 2 * n), :], gz_r.at[4 + k]).wait_recv()
        for half in range(2):
            rows = pl.ds(half * 128 + k * n, n)
            send(raw.at[6, rows, :], raw.at[7, rows, :], None, gx_r.at[5], xp(2))

    arrive = {
        1: lambda: gx[3].wait_recv(),
        2: lambda: gx[2].wait_recv(),
        3: lambda: [c.wait_recv() for c in far["x"]],
        4: lambda: [forward_x(), forward_z(0)],
        5: lambda: [gz[2].wait_recv(), gz[3].wait_recv()],
        6: lambda: None,
        7: lambda: Group(raw.at[7], gx_r.at[5]).wait_recv(),
    }

    def need(k):
        if k not in oc:
            arrive[k]()
            oc[k] = normalize(k)

    piece = pl.multiple_of(y * 64, 64)
    nt = (((1,), (1,)), ((), ()))
    eye = (
        lax.broadcasted_iota(jnp.int32, (256, 256), 0) == lax.broadcasted_iota(jnp.int32, (256, 256), 1)
    )

    ry, zx, ay = {}, {}, {}
    mine = pl.ds(piece, 64)

    def rows_of(d, at=0, n=64):
        return pl.ds(pl.multiple_of(((y + d) % 4) * 64 + at, 32), n)

    def blocks_of(u):
        i, j = UNITS[u]
        return (0, 7) if (i, j) == (3, 3) else (i, 3 + j if j else 0)

    def stage0(u):
        i, j = UNITS[u]
        row, col = blocks_of(u)
        need(col)
        need(row)
        g = lax.dot_general(nrm[row], nrm[col], nt, preferred_element_type=f32)
        if i == 0 and j == 0:
            g = jnp.where(eye, g - WIDTH / 8, g)
        gp[i, j] = g.astype(bf16)
        if u < RING:
            for half, to in ((0, 1), (1, 3)):
                src = gp.at[i, j, rows_of(2, half * 32, 32), :]
                send(src, rsy.at[2, i, j, pl.ds(half * 32, 32), :], None, y_r.at[u, 0], yp(to))
            ry[u] = Group(rsy.at[2, i, j], y_r.at[u, 0])
        else:
            for d in (2, 1, 3):
                send(gp.at[i, j, rows_of(d), :], rsy.at[d - 1, i, j], None, y_r.at[u, 1], yp(d))
            ry[u] = Group(rsy.at[:, i, j], y_r.at[u, 1])

    def relay_y(u):
        i, j = UNITS[u]
        ry[u].wait_recv()
        up = rsy[2, i, j, 0:32, :].astype(f32) + gp[i, j, rows_of(1, 0, 32), :].astype(f32)
        ps[0, i, j, 0:32, :] = up.astype(bf16)
        ps[0, i, j, 32:64, :] = gp[i, j, rows_of(1, 32, 32), :]
        down = rsy[2, i, j, 32:64, :].astype(f32) + gp[i, j, rows_of(3, 32, 32), :].astype(f32)
        ps[1, i, j, 0:32, :] = gp[i, j, rows_of(3, 0, 32), :]
        ps[1, i, j, 32:64, :] = down.astype(bf16)
        for k in range(2):
            send(ps.at[k, i, j], rsy.at[k, i, j], None, y_r.at[u, 1], yp(1 + 2 * k))
        ry[u] = Group(rsy.at[0:2, i, j], y_r.at[u, 1])

    def stage1(u):
        i, j = UNITS[u]
        ry[u].wait_recv()
        total = gp[i, j, mine, :].astype(f32)
        for k in range(2 if u < RING else 3):
            total = total + rsy[k, i, j].astype(f32)
        zs[i, j] = total.astype(bf16)
        zx[u] = send(zs.at[i, j], rz.at[i, j], None, z_r.at[u], lp)

    def stage2(u):
        i, j = UNITS[u]
        zx[u].wait_recv()
        gf[i, j, mine, :] = (zs[i, j].astype(f32) + rz[i, j].astype(f32)).astype(bf16)
        at = gf.at[i, j, mine, :]
        send(at, pc.at[u], None, pc_r.at[0], cp)
        for d in (1, 3) if u < RING else (2, 1, 3):
            send(at, at, None, ay_r.at[u, 0], yp(d))
        ay[u] = Group(rsy.at[0:2, i, j] if u < RING else rsy.at[:, i, j], ay_r.at[u, 0])

    def pass_y(u):
        i, j = UNITS[u]
        ay[u].wait_recv()
        a = gf.at[i, j, rows_of(3, 0, 32), :]
        b = gf.at[i, j, rows_of(1, 32, 32), :]
        send(a, a, None, ay_r.at[u, 1], yp(1))
        send(b, b, None, ay_r.at[u, 1], yp(3))
        ay[u] = Group(rsy.at[2, i, j], ay_r.at[u, 1])

    def step_own(i, acc):
        at = pl.ds(pl.multiple_of(core * 128 + i * 32, 32), 32)
        m, o = nrm[0, at, :].astype(f32), oth[0, at, :].astype(f32)
        return tuple(
            q + jnp.sum(v.reshape(4, 8, 1024), axis=0) for q, v in zip(acc, (m * o, m, o, m * m, o * o))
        )

    def hop(src, buf, me, rs, to):
        buf[me] = src[...]
        for d in (1, 2, 3):
            send(buf.at[me], buf.at[me], None, rs.at[0], to(d))
        return [Group(buf.at[0:3], rs.at[0])]

    def swap_cores(src, buf, rs):
        buf[core] = src[...]
        return [send(buf.at[core], buf.at[core], None, rs.at[0], cp)]

    def gathered(dst, buf, n, cs):
        for c in cs:
            c.wait_recv()
        total = buf[0]
        for k in range(1, n):
            total = total + buf[k]
        dst[...] = total

    pend = {}

    def own0():
        oc[0].wait_recv()
        ab, sm, so, mm, oo = (
            jnp.sum(v, axis=0, keepdims=True)
            for v in lax.fori_loop(0, 4, step_own, (jnp.zeros((8, 1024), f32),) * 5)
        )
        rows = (
            ab, jnp.where(first, sm, so), jnp.where(first, so, sm),
            jnp.where(first, mm, oo), jnp.where(first, oo, mm),
        )
        for k, v in enumerate(rows):
            own[k : k + 1, :] = v
        own[5:8, :] = jnp.zeros((3, 1024), f32)
        pend["own"] = hop(own, ox, x, ox_r, xp)

    def own1():
        gathered(own, ox, 4, pend["own"])
        pend["own"] = swap_cores(own, oc2, o_r)

    def own2():
        gathered(own, oc2, 2, pend["own"])
        pend["own"] = hop(own, oz, zh, oz_r, zp)

    def own3():
        gathered(own, oz, 4, pend["own"])

    scale = 2.0 * lam / BATCH

    def loss0():
        Group(pc, pc_r.at[0]).wait_recv()
        acc = jnp.zeros((8, 256), f32)
        for u, (i, j) in enumerate(UNITS):
            g, h = gf[i, j, mine, :].astype(f32), pc[u].astype(f32)
            if i == 0 and j == 0:
                here = lax.broadcasted_iota(jnp.int32, (64, 256), 0) + piece
                here = here == lax.broadcasted_iota(jnp.int32, (64, 256), 1)
                g, h = jnp.where(here, g + WIDTH, g), jnp.where(here, h + WIDTH, h)
            p = jnp.sum((g * h).reshape(8, 8, 256), axis=0)
            acc = acc + (2.0 * p if (i, j) == (1, 0) else p)
        pairs = jnp.sum(jnp.sum(acc, axis=0, keepdims=True), axis=1, keepdims=True) / (BATCH * BATCH)
        cii = own[0:1, :] / BATCH
        terms = jnp.sum((1.0 - cii) * (1.0 - cii) - lam * cii * cii, axis=1, keepdims=True)
        ly[ft] = jnp.broadcast_to(0.25 * lam * pairs + terms / 32.0, (8, 128))
        for k in (1, 2, 3):
            send(ly.at[ft], ly.at[ft], None, ly_r.at[0], yp(k))
            send(ly.at[ft], ly.at[ft], None, ly_r.at[0], yq(k))
        send(ly.at[ft], ly.at[ft], None, ly_r.at[0], lp)

    def loss1():
        lme = zh * 2 + core
        gathered(lz.at[lme], ly, 8, [Group(ly.at[0:7], ly_r.at[0])])
        for k in (1, 2, 3):
            send(lz.at[lme], lz.at[lme], None, lz_r.at[0], zp(k))
            send(lz.at[lme], lz.at[lme], None, lz_r.at[0], zq(k))
        send(lz.at[lme], lz.at[lme], None, lz_r.at[0], cp)

    def loss2():
        gathered(lsum, lz, 8, [Group(lz.at[0:7], lz_r.at[0])])
        pend["loss"] = hop(lsum, lx, x, lx_r, xp)

    mom[...] = jnp.zeros((2, 1024), f32)
    tn = (((0,), (0,)), ((), ()))
    nn = (((1,), (0,)), ((), ()))

    def product(i, terms, store):
        def tile(t, _):
            cols = pl.ds(pl.multiple_of(t * 256, 256), 256)
            acc = jnp.zeros((256, 256), f32)
            for p, q, k, how in terms:
                acc = acc + lax.dot_general(gf[p, q], oth[k, :, cols], how, preferred_element_type=f32)
            mom[0:1, cols] += jnp.sum(acc, axis=0, keepdims=True)
            mom[1:2, cols] += jnp.sum(acc * oth[i, :, cols].astype(f32), axis=0, keepdims=True)
            store(cols, acc)
            return 0

        lax.fori_loop(0, 4, tile, 0)

    def upper(i):
        terms = [(i, j, 3 + j if j else 0, nn) for j in range(4) if (i, j) in UNITS and (i, j) != (3, 3)]

        def store(cols, acc):
            if i == 0:
                u0[:, cols] = acc
            else:
                us[i, :, cols] = acc.astype(bf16)
            if i in (1, 2):
                uf[i - 1, :, cols] = acc

        product(i, terms + [(1, 0, 1, tn)] if i == 0 else terms, store)

    def upper_far():
        def store(cols, acc):
            acc = acc + u0[:, cols]
            u0[:, cols] = acc
            us[0, :, cols] = acc.astype(bf16)

        product(0, [(3, 3, 7, nn)], store)

    same, diff = [], []
    got = set()

    def stage3(u):
        ay[u].wait_recv()
        got.add(UNITS[u])
        i, j = UNITS[u]
        for k in blocks_of(u) + (1,):
            if k not in ready and k in oc:
                ready.add(k)
                oc[k].wait_recv()
        if (i, j) == (3, 3):
            upper_far()
            diff.append(send(us.at[0, pl.ds(rows_o, 128), :], rs_diff.at[0], ud_s.at[0], ud_r.at[0], cp))
            return
        if not all(v in got for v in UNITS if v[0] == i and v != (3, 3)):
            return
        upper(i)
        rows_same, rows_diff = pl.ds(rows_c, 128), pl.ds(rows_o, 128)
        if i == 3:
            relays.append(send(us.at[3, rows_same, :], relay.at[0], rl_s.at[0], rl_r.at[0], xp(1)))
            relays.append(send(us.at[3, rows_diff, :], relay.at[1], rl_s.at[1], rl_r.at[1], xp(3)))
        elif i == 1:
            diff.append(send(us.at[1, rows_diff, :], rs_diff.at[1], ud_s.at[1], ud_r.at[1], xq(1)))
        elif i == 2:
            same.append(send(us.at[2, rows_same, :], rs_same.at[1], us_s.at[1], us_r.at[1], xp(3)))

    def pass_x(k):
        start = rows_o if k else rows_c
        relays[k].wait_recv()

        def add(t, _):
            r = pl.ds(pl.multiple_of(t * 32, 32), 32)
            at = pl.ds(pl.multiple_of(start + t * 32, 32), 32)
            us[k + 1, at, :] = (uf[k, at, :] + relay[k, r, :].astype(f32)).astype(bf16)
            return 0

        lax.fori_loop(0, 4, add, 0)
        src = us.at[k + 1, pl.ds(start, 128), :]
        if k == 0:
            same.append(send(src, rs_same.at[0], us_s.at[0], us_r.at[0], xp(1)))
        else:
            diff.append(send(src, rs_diff.at[2], ud_s.at[2], ud_r.at[2], xq(3)))

    relays = []
    ready = {0}
    stages = (stage0, relay_y, stage1, stage2, pass_y, stage3)
    owns = (own0, own1, own2, own3, loss0)
    for stage, u in ORDER:
        if stage < 6:
            stages[stage](u)
        elif stage == 6:
            forward_z(u)
        elif stage == 8:
            pass_far(u)
        elif stage == 10:
            pass_x(u)
        else:
            owns[u]()

    mz_wait = hop(mom, mz, zh, mz_r, zp)
    cst.wait_recv()
    ab, s_a, s_b, aa, bb = (own[k : k + 1, :] for k in range(5))
    cii = ab / BATCH
    d = (2.0 * (cii - 1.0)).astype(bf16).astype(f32) - 2.0 * lam * cii
    xme = x * 2 + core
    loss1()
    gathered(mx.at[xme], mz, 4, mz_wait)
    for k in (1, 2, 3):
        send(mx.at[xme], mx.at[xme], None, mx_r.at[0], xp(k))
        send(mx.at[xme], mx.at[xme], None, mx_r.at[0], xq(k))
    send(mx.at[xme], mx.at[xme], None, mx_r.at[0], cp)
    loss2()
    Group(mx.at[0:7], mx_r.at[0]).wait_recv()
    b_sums = mx[0] + mx[2] + mx[4] + mx[6]
    a_sums = mx[1] + mx[3] + mx[5] + mx[7]
    first_b, quad_b, first_a, quad_a = b_sums[0:1], b_sums[1:2], a_sums[0:1], a_sums[1:2]
    one_a = (scale * (first_a + WIDTH * s_a) + d * s_b) / BATCH
    one_b = (scale * (first_b + WIDTH * s_b) + d * s_a) / BATCH
    two_a = (scale * (quad_a + WIDTH * aa) + d * ab) / BATCH
    two_b = (scale * (quad_b + WIDTH * bb) + d * ab) / BATCH
    one_m, two_m = jnp.where(first, one_a, one_b), jnp.where(first, two_a, two_b)
    one_c, two_c = jnp.where(first, one_b, one_a), jnp.where(first, two_b, two_a)
    for c in same + diff:
        c.wait_recv()

    def finish(i, _):
        r = pl.ds(pl.multiple_of(i * 32, 32), 32)
        at = pl.ds(pl.multiple_of(core * 128 + i * 32, 32), 32)
        m, o = nrm[0, at, :].astype(f32), oth[0, at, :].astype(f32)
        up_c = u0[at, :] + rs_same[0, r, :].astype(f32) + rs_same[1, r, :].astype(f32)
        up_m = rs_diff[0, r, :].astype(f32) + rs_diff[1, r, :].astype(f32) + rs_diff[2, r, :].astype(f32)
        up_c = scale * (up_c + WIDTH * o) + d * m
        up_m = scale * (up_m + WIDTH * m) + d * o
        grad_m = st_mine[1:2, :] * (up_m - one_m - m * two_m)
        grad_c = st_cross[1:2, :] * (up_c - one_c - o * two_c)
        ga_ref[r, :] = jnp.where(first, grad_m, grad_c)
        gb_ref[r, :] = jnp.where(first, grad_c, grad_m)
        return 0

    lax.fori_loop(0, 4, finish, 0)
    gathered(lsum, lx, 4, pend["loss"])
    loss_ref[...] = lsum[0:1, 0:1]
    for c in sends + list(busy.values()):
        c.wait_send()


def local(view_a, view_b):
    dma = pltpu.SemaphoreType.DMA
    vm = pltpu.VMEM
    sems = [
        dma(shape)
        for shape in (
            (2,), (POOL,), (2,), (6,), (4 + 2 * PARTS,), (8,), (2,), (3,), (2,),
            (2,), (6,), (4 + PARTS,), (8,), (2,), (3,), (2,), (NU, 2), (NU,), (NU, 2),
        )
    ] + [dma((1,))] * 11
    vmem = pl.BlockSpec(memory_space=pltpu.VMEM)
    loss, grad_a, grad_b = pl.pallas_call(
        kernel,
        out_shape=(
            jax.ShapeDtypeStruct((1, 1), f32),
            jax.ShapeDtypeStruct((128, 1024), f32),
            jax.ShapeDtypeStruct((128, 1024), f32),
        ),
        in_specs=[pl.BlockSpec(memory_space=pltpu.HBM)] * 2,
        out_specs=(vmem, vmem, vmem),
        scratch_shapes=[
            vm((128, 1024), bf16), vm((128, 1024), bf16),
            vm((8, 256, 1024), bf16), vm((8, 256, 1024), bf16), vm((8, 256, 1024), bf16),
            vm((128, 1024), bf16),
            vm((4, 2, 1024), f32), vm((4, 2, 1024), f32), vm((8, 1024), f32), vm((8, 1024), f32),
            vm((4, 4, 256, 256), bf16), vm((3, 4, 4, 64, 256), bf16), vm((2, 4, 4, 64, 256), bf16),
            vm((4, 4, 64, 256), bf16), vm((4, 4, 64, 256), bf16),
            vm((4, 4, 256, 256), bf16),
            vm((4, 256, 1024), bf16), vm((256, 1024), f32),
            vm((2, 256, 1024), f32), vm((2, 128, 1024), bf16),
            vm((2, 128, 1024), bf16), vm((3, 128, 1024), bf16),
            vm((2, 1024), f32), vm((8, 2, 1024), f32), vm((4, 2, 1024), f32), vm((NU, 64, 256), bf16),
            vm((8, 1024), f32), vm((4, 8, 1024), f32), vm((4, 8, 1024), f32), vm((2, 8, 1024), f32),
            vm((8, 8, 128), f32), vm((8, 8, 128), f32), vm((4, 8, 128), f32), vm((8, 128), f32),
        ] + sems,
        compiler_params=pltpu.CompilerParams(
            collective_id=0, has_side_effects=True, vmem_limit_bytes=54 * 2**20
        ),
        name="twins",
    )(view_a, view_b)
    return loss[0, 0], grad_a, grad_b


def solution(mesh):
    placed = (P("dp", "feat"), P("dp", "feat"))
    return jax.shard_map(
        local,
        mesh=mesh,
        in_specs=placed,
        out_specs=(P(), P("dp", "feat"), P("dp", "feat")),
        check_vma=False,
    )
```

```python
import jax
import jax.numpy as jnp
from jax import lax
from jax.experimental import pallas as pl
from jax.experimental.pallas import tpu as pltpu
from jax.sharding import PartitionSpec as P

lam = 0.0051
eps = 1e-05
BATCH = 4096.0
WIDTH = 8192.0
MESH = pl.DeviceIdType.MESH
f32 = jnp.float32
bf16 = jnp.bfloat16

OFF = (0, 1, 3, 2)

UNITS = (
    (0, 0), (0, 1), (1, 0), (1, 1), (2, 1), (3, 0), (3, 1), (3, 2),
    (1, 2), (2, 2), (0, 2), (1, 3), (2, 3), (0, 3), (3, 3),
)
NU = len(UNITS)
RING = 11
ORDER = (
    (0, 0), (1, 0), (2, 0), (0, 1), (0, 2), (0, 3), (0, 4), (6, 1), (1, 1), (1, 2),
    (1, 3), (0, 5), (1, 4), (0, 6), (7, 0), (6, 2), (2, 1), (2, 2), (2, 3), (1, 5),
    (6, 3), (2, 4), (1, 6), (8, 0), (3, 0), (0, 7), (2, 5), (6, 4), (7, 1), (8, 1),
    (2, 6), (8, 2), (4, 0), (3, 1), (0, 8), (1, 7), (6, 5), (3, 2), (0, 9), (3, 3),
    (0, 10), (5, 0), (8, 3), (4, 1), (3, 4), (6, 6), (1, 8), (3, 5), (2, 7), (4, 2),
    (1, 9), (8, 4), (4, 3), (3, 6), (1, 10), (6, 7), (5, 1), (4, 4), (8, 5), (2, 8),
    (4, 5), (5, 2), (8, 6), (3, 7), (2, 9), (5, 3), (4, 6), (8, 7), (7, 2), (0, 11),
    (2, 10), (3, 8), (5, 4), (0, 12), (5, 5), (0, 13), (4, 7), (3, 9), (5, 6), (3, 10),
    (2, 11), (0, 14), (4, 8), (2, 12), (2, 13), (3, 11), (5, 7), (4, 9), (4, 10), (3, 12),
    (2, 14), (5, 8), (3, 13), (5, 11), (5, 9), (5, 10), (3, 14), (5, 12), (5, 13), (7, 3),
    (7, 4), (10, 0), (10, 1), (5, 14),
)
POOL = 48
PARTS = 8


def kernel(
    va_hbm, vb_hbm, loss_ref, rstd_ref, ga_ref, gb_ref,
    va, vb, raw, nrm, oth, swap, st_x, st_z, st_mine, st_cross,
    gp, rsy, ps, zs, rz, gf, us, u0, uf, relay, rs_same, rs_diff,
    mom, mx, mz, pc, own, ox, oz, oc2, ly, lz, lx, lsum,
    in_s, pool_s, core_s, gx_s, gz_s, oth_s, us_s, ud_s, rl_s,
    core_r, gx_r, gz_r, oth_r, us_r, ud_r, rl_r, y_r, z_r, ay_r,
    sx_r, sz_r, mx_r, mz_r, pc_r, ox_r, oz_r, o_r, ly_r, lz_r, lx_r,
):
    dp = lax.axis_index("dp")
    ft = lax.axis_index("feat")
    x, zh, core = dp // 8, (dp // 2) % 4, dp % 2
    y, zl = ft // 2, ft % 2

    def dev(ax, az, ac, ay, al):
        return (ax * 8 + az * 2 + ac, ay * 2 + al)

    def xp(d):
        return dev((x + d) % 4, zh, core, y, zl)

    def xq(d):
        return dev((x + d) % 4, zh, 1 - core, y, zl)

    def zp(d):
        return dev(x, (zh + d) % 4, core, y, zl)

    def yp(d):
        return dev(x, zh, core, (y + d) % 4, zl)

    def zq(d):
        return dev(x, (zh + d) % 4, 1 - core, y, zl)

    def yq(d):
        return dev(x, zh, core, (y + d) % 4, 1 - zl)

    cp = dev(x, zh, 1 - core, y, zl)
    lp = dev(x, zh, core, y, 1 - zl)

    sends, busy, turn = [], {}, [0]

    def send(src, dst, ss, rs, to):
        slot = None
        if ss is None:
            slot = turn[0] % POOL
            turn[0] += 1
            if slot in busy:
                busy[slot].wait_send()
            ss = pool_s.at[slot]
        c = pltpu.make_async_remote_copy(
            src_ref=src, dst_ref=dst, send_sem=ss, recv_sem=rs, device_id=to, device_id_type=MESH
        )
        c.start()
        if slot is None:
            sends.append(c)
        else:
            busy[slot] = c
        return c

    class Group:
        def __init__(self, buf, rs):
            self.buf, self.rs = buf, rs

        def wait_recv(self):
            pltpu.make_async_remote_copy(
                src_ref=self.buf, dst_ref=self.buf, send_sem=pool_s.at[0], recv_sem=self.rs,
                device_id=cp, device_id_type=MESH,
            ).wait_recv()

    loads = [
        pltpu.make_async_copy(src, dst, in_s.at[k])
        for k, (src, dst) in enumerate(((va_hbm, va), (vb_hbm, vb)))
    ]
    for c in loads:
        c.start()
    barrier = pltpu.get_barrier_semaphore()
    peers = [cp, lp]
    for d in (1, 2, 3):
        peers += [xp(d), xq(d), zp(d), zq(d), yp(d), yq(d)]
    for p in peers:
        pl.semaphore_signal(barrier, inc=1, device_id=p, device_id_type=MESH)

    first = core == 0
    rows_c = pl.multiple_of(core * 128, 128)
    rows_o = pl.multiple_of((1 - core) * 128, 128)

    for c in loads:
        c.wait()

    def split(i, _):
        r = pl.ds(pl.multiple_of(i * 32, 32), 32)
        a, b = va[r, :], vb[r, :]
        raw[0, pl.ds(pl.multiple_of(core * 128 + i * 32, 32), 32), :] = jnp.where(first, a, b)
        swap[r, :] = jnp.where(first, b, a)
        return 0

    lax.fori_loop(0, 4, split, 0)
    pl.semaphore_wait(barrier, len(peers))

    c = send(swap, raw.at[0, pl.ds(rows_c, 128), :], core_s.at[0], core_r.at[0], cp)
    c.wait_recv()

    lo, hi = pl.ds(0, 128), pl.ds(128, 128)
    own_lo, own_hi = raw.at[0, lo, :], raw.at[0, hi, :]

    def ring(next_lo, next_hi, prev_lo, prev_hi, ss, rs, to):
        return (
            send(own_lo, prev_lo, ss.at[0], rs.at[0], to(1)),
            send(own_hi, next_hi, ss.at[1], rs.at[1], to(3)),
            send(own_hi, prev_hi, ss.at[2], rs.at[2], to(1)),
            send(own_lo, next_lo, ss.at[3], rs.at[3], to(3)),
        )

    def forward(prev_lo, next_hi, far, ss, rs, to, near):
        near[0].wait_recv()
        send(prev_lo, raw.at[far, lo, :], ss.at[4], rs.at[4], to(1))
        near[1].wait_recv()
        send(next_hi, raw.at[far, hi, :], ss.at[5], rs.at[4], to(3))
        return [Group(raw.at[far], rs.at[4])]

    def sums(i, acc):
        v = raw[0, pl.ds(pl.multiple_of(i * 32, 32), 32), :].astype(f32)
        return acc + jnp.sum(v.reshape(4, 8, 1024), axis=0)

    mean = jnp.sum(lax.fori_loop(0, 8, sums, jnp.zeros((8, 1024), f32)), axis=0, keepdims=True) / 256.0

    def squares(i, acc):
        v = raw[0, pl.ds(pl.multiple_of(i * 32, 32), 32), :].astype(f32) - mean
        return acc + jnp.sum((v * v).reshape(4, 8, 1024), axis=0)

    m2 = jnp.sum(lax.fori_loop(0, 8, squares, jnp.zeros((8, 1024), f32)), axis=0, keepdims=True)

    def combine(buf, count):
        means = [buf[k, 0:1, :] for k in range(4)]
        avg = (means[0] + means[1] + means[2] + means[3]) * 0.25
        total = buf[0, 1:2, :] + buf[1, 1:2, :] + buf[2, 1:2, :] + buf[3, 1:2, :]
        dev2 = sum((m - avg) * (m - avg) for m in means)
        return avg, total + count * dev2

    def spread(value_a, value_b, buf, me, rs, to):
        buf[me, 0:1, :] = value_a
        buf[me, 1:2, :] = value_b
        for d in (1, 2, 3):
            send(buf.at[me], buf.at[me], None, rs.at[0], to(d))
        return [Group(buf.at[0:3], rs.at[0])]

    sz = spread(mean, m2, st_z, zh, sz_r, zp)
    gz = ring(
        raw.at[5, lo, :], raw.at[4, lo, :], raw.at[4, hi, :], raw.at[5, hi, :], gz_s, gz_r, zp
    )
    for c in sz:
        c.wait_recv()
    mean, m2 = combine(st_z, 256.0)
    sx = spread(mean, m2, st_x, x, sx_r, xp)
    gx = ring(
        raw.at[1, lo, :], raw.at[1, hi, :], raw.at[2, lo, :], raw.at[2, hi, :], gx_s, gx_r, xp
    )
    for c in sx:
        c.wait_recv()
    mean, m2 = combine(st_x, 1024.0)
    rstd = lax.rsqrt(m2 / BATCH + eps)
    st_mine[0:1, :] = mean
    st_mine[1:2, :] = rstd
    cst = send(st_mine, st_cross, core_s.at[1], core_r.at[1], cp)

    def normalize(k):
        def step(i, _):
            r = pl.ds(pl.multiple_of(i * 32, 32), 32)
            v = raw[k, r, :].astype(f32)
            nrm[k, r, :] = ((v - st_mine[0:1, :]) * st_mine[1:2, :]).astype(bf16)
            return 0

        lax.fori_loop(0, 8, step, 0)
        return send(nrm.at[k], oth.at[k], oth_s.at[k], oth_r.at[k], cp)

    oc = {0: normalize(0)}
    far = {}

    def forward_x():
        far["x"] = forward(raw.at[2, lo, :], raw.at[1, hi, :], 3, gx_s, gx_r, xp, gx)

    def forward_z(k):
        if k >= PARTS:
            return
        n = 128 // PARTS
        for e, (half, to) in enumerate(((1, 1), (0, 3))):
            if k == 0:
                gz[e].wait_recv()
            src = raw.at[4, pl.ds(half * 128 + k * n, n), :]
            dst = raw.at[6, pl.ds((1 - half) * 128 + k * n, n), :]
            send(src, dst, gz_s.at[4 + 2 * k + e], gz_r.at[4 + k], zp(to))

    def pass_far(k):
        n = 128 // PARTS
        Group(raw.at[6, pl.ds(0, 2 * n), :], gz_r.at[4 + k]).wait_recv()
        for half in range(2):
            rows = pl.ds(half * 128 + k * n, n)
            send(raw.at[6, rows, :], raw.at[7, rows, :], None, gx_r.at[5], xp(2))

    arrive = {
        1: lambda: gx[3].wait_recv(),
        2: lambda: gx[2].wait_recv(),
        3: lambda: [c.wait_recv() for c in far["x"]],
        4: lambda: [forward_x(), forward_z(0)],
        5: lambda: [gz[2].wait_recv(), gz[3].wait_recv()],
        6: lambda: None,
        7: lambda: Group(raw.at[7], gx_r.at[5]).wait_recv(),
    }

    def need(k):
        if k not in oc:
            arrive[k]()
            oc[k] = normalize(k)

    piece = pl.multiple_of(y * 64, 64)
    nt = (((1,), (1,)), ((), ()))
    eye = (
        lax.broadcasted_iota(jnp.int32, (256, 256), 0) == lax.broadcasted_iota(jnp.int32, (256, 256), 1)
    )

    ry, zx, ay = {}, {}, {}
    mine = pl.ds(piece, 64)

    def rows_of(d, at=0, n=64):
        return pl.ds(pl.multiple_of(((y + d) % 4) * 64 + at, 32), n)

    def blocks_of(u):
        i, j = UNITS[u]
        return (0, 7) if (i, j) == (3, 3) else (i, 3 + j if j else 0)

    def stage0(u):
        i, j = UNITS[u]
        row, col = blocks_of(u)
        need(col)
        need(row)
        g = lax.dot_general(nrm[row], nrm[col], nt, preferred_element_type=f32)
        if i == 0 and j == 0:
            g = jnp.where(eye, g - WIDTH / 8, g)
        gp[i, j] = g.astype(bf16)
        if u < RING:
            for half, to in ((0, 1), (1, 3)):
                src = gp.at[i, j, rows_of(2, half * 32, 32), :]
                send(src, rsy.at[2, i, j, pl.ds(half * 32, 32), :], None, y_r.at[u, 0], yp(to))
            ry[u] = Group(rsy.at[2, i, j], y_r.at[u, 0])
        else:
            for d in (2, 1, 3):
                send(gp.at[i, j, rows_of(d), :], rsy.at[d - 1, i, j], None, y_r.at[u, 1], yp(d))
            ry[u] = Group(rsy.at[:, i, j], y_r.at[u, 1])

    def relay_y(u):
        i, j = UNITS[u]
        ry[u].wait_recv()
        up = rsy[2, i, j, 0:32, :].astype(f32) + gp[i, j, rows_of(1, 0, 32), :].astype(f32)
        ps[0, i, j, 0:32, :] = up.astype(bf16)
        ps[0, i, j, 32:64, :] = gp[i, j, rows_of(1, 32, 32), :]
        down = rsy[2, i, j, 32:64, :].astype(f32) + gp[i, j, rows_of(3, 32, 32), :].astype(f32)
        ps[1, i, j, 0:32, :] = gp[i, j, rows_of(3, 0, 32), :]
        ps[1, i, j, 32:64, :] = down.astype(bf16)
        for k in range(2):
            send(ps.at[k, i, j], rsy.at[k, i, j], None, y_r.at[u, 1], yp(1 + 2 * k))
        ry[u] = Group(rsy.at[0:2, i, j], y_r.at[u, 1])

    def stage1(u):
        i, j = UNITS[u]
        ry[u].wait_recv()
        total = gp[i, j, mine, :].astype(f32)
        for k in range(2 if u < RING else 3):
            total = total + rsy[k, i, j].astype(f32)
        zs[i, j] = total.astype(bf16)
        zx[u] = send(zs.at[i, j], rz.at[i, j], None, z_r.at[u], lp)

    def stage2(u):
        i, j = UNITS[u]
        zx[u].wait_recv()
        gf[i, j, mine, :] = (zs[i, j].astype(f32) + rz[i, j].astype(f32)).astype(bf16)
        at = gf.at[i, j, mine, :]
        send(at, pc.at[u], None, pc_r.at[0], cp)
        for d in (1, 3) if u < RING else (2, 1, 3):
            send(at, at, None, ay_r.at[u, 0], yp(d))
        ay[u] = Group(rsy.at[0:2, i, j] if u < RING else rsy.at[:, i, j], ay_r.at[u, 0])

    def pass_y(u):
        i, j = UNITS[u]
        ay[u].wait_recv()
        a = gf.at[i, j, rows_of(3, 0, 32), :]
        b = gf.at[i, j, rows_of(1, 32, 32), :]
        send(a, a, None, ay_r.at[u, 1], yp(1))
        send(b, b, None, ay_r.at[u, 1], yp(3))
        ay[u] = Group(rsy.at[2, i, j], ay_r.at[u, 1])

    def step_own(i, acc):
        at = pl.ds(pl.multiple_of(core * 128 + i * 32, 32), 32)
        m, o = nrm[0, at, :].astype(f32), oth[0, at, :].astype(f32)
        return tuple(
            q + jnp.sum(v.reshape(4, 8, 1024), axis=0) for q, v in zip(acc, (m * o, m, o, m * m, o * o))
        )

    def hop(src, buf, me, rs, to):
        buf[me] = src[...]
        for d in (1, 2, 3):
            send(buf.at[me], buf.at[me], None, rs.at[0], to(d))
        return [Group(buf.at[0:3], rs.at[0])]

    def swap_cores(src, buf, rs):
        buf[core] = src[...]
        return [send(buf.at[core], buf.at[core], None, rs.at[0], cp)]

    def gathered(dst, buf, n, cs):
        for c in cs:
            c.wait_recv()
        total = buf[0]
        for k in range(1, n):
            total = total + buf[k]
        dst[...] = total

    pend = {}

    def own0():
        oc[0].wait_recv()
        ab, sm, so, mm, oo = (
            jnp.sum(v, axis=0, keepdims=True)
            for v in lax.fori_loop(0, 4, step_own, (jnp.zeros((8, 1024), f32),) * 5)
        )
        rows = (
            ab, jnp.where(first, sm, so), jnp.where(first, so, sm),
            jnp.where(first, mm, oo), jnp.where(first, oo, mm),
        )
        for k, v in enumerate(rows):
            own[k : k + 1, :] = v
        own[5:8, :] = jnp.zeros((3, 1024), f32)
        pend["own"] = hop(own, ox, x, ox_r, xp)

    def own1():
        gathered(own, ox, 4, pend["own"])
        pend["own"] = swap_cores(own, oc2, o_r)

    def own2():
        gathered(own, oc2, 2, pend["own"])
        pend["own"] = hop(own, oz, zh, oz_r, zp)

    def own3():
        gathered(own, oz, 4, pend["own"])

    scale = 2.0 * lam / BATCH

    def loss0():
        Group(pc, pc_r.at[0]).wait_recv()
        acc = jnp.zeros((8, 256), f32)
        for u, (i, j) in enumerate(UNITS):
            g, h = gf[i, j, mine, :].astype(f32), pc[u].astype(f32)
            if i == 0 and j == 0:
                here = lax.broadcasted_iota(jnp.int32, (64, 256), 0) + piece
                here = here == lax.broadcasted_iota(jnp.int32, (64, 256), 1)
                g, h = jnp.where(here, g + WIDTH, g), jnp.where(here, h + WIDTH, h)
            p = jnp.sum((g * h).reshape(8, 8, 256), axis=0)
            acc = acc + (2.0 * p if (i, j) == (1, 0) else p)
        pairs = jnp.sum(jnp.sum(acc, axis=0, keepdims=True), axis=1, keepdims=True) / (BATCH * BATCH)
        cii = own[0:1, :] / BATCH
        terms = jnp.sum((1.0 - cii) * (1.0 - cii) - lam * cii * cii, axis=1, keepdims=True)
        ly[ft] = jnp.broadcast_to(0.25 * lam * pairs + terms / 32.0, (8, 128))
        for k in (1, 2, 3):
            send(ly.at[ft], ly.at[ft], None, ly_r.at[0], yp(k))
            send(ly.at[ft], ly.at[ft], None, ly_r.at[0], yq(k))
        send(ly.at[ft], ly.at[ft], None, ly_r.at[0], lp)

    def loss1():
        lme = zh * 2 + core
        gathered(lz.at[lme], ly, 8, [Group(ly.at[0:7], ly_r.at[0])])
        for k in (1, 2, 3):
            send(lz.at[lme], lz.at[lme], None, lz_r.at[0], zp(k))
            send(lz.at[lme], lz.at[lme], None, lz_r.at[0], zq(k))
        send(lz.at[lme], lz.at[lme], None, lz_r.at[0], cp)

    def loss2():
        gathered(lsum, lz, 8, [Group(lz.at[0:7], lz_r.at[0])])
        pend["loss"] = hop(lsum, lx, x, lx_r, xp)

    mom[...] = jnp.zeros((2, 1024), f32)
    tn = (((0,), (0,)), ((), ()))
    nn = (((1,), (0,)), ((), ()))

    def product(i, terms, store):
        def tile(t, _):
            cols = pl.ds(pl.multiple_of(t * 256, 256), 256)
            acc = jnp.zeros((256, 256), f32)
            for p, q, k, how in terms:
                acc = acc + lax.dot_general(gf[p, q], oth[k, :, cols], how, preferred_element_type=f32)
            mom[0:1, cols] += jnp.sum(acc, axis=0, keepdims=True)
            mom[1:2, cols] += jnp.sum(acc * oth[i, :, cols].astype(f32), axis=0, keepdims=True)
            store(cols, acc)
            return 0

        lax.fori_loop(0, 4, tile, 0)

    def upper(i):
        terms = [(i, j, 3 + j if j else 0, nn) for j in range(4) if (i, j) in UNITS and (i, j) != (3, 3)]

        def store(cols, acc):
            if i == 0:
                u0[:, cols] = acc
            else:
                us[i, :, cols] = acc.astype(bf16)
            if i in (1, 2):
                uf[i - 1, :, cols] = acc

        product(i, terms + [(1, 0, 1, tn)] if i == 0 else terms, store)

    def upper_far():
        def store(cols, acc):
            acc = acc + u0[:, cols]
            u0[:, cols] = acc
            us[0, :, cols] = acc.astype(bf16)

        product(0, [(3, 3, 7, nn)], store)

    same, diff = [], []
    got = set()

    def stage3(u):
        ay[u].wait_recv()
        got.add(UNITS[u])
        i, j = UNITS[u]
        for k in blocks_of(u) + (1,):
            if k not in ready and k in oc:
                ready.add(k)
                oc[k].wait_recv()
        if (i, j) == (3, 3):
            upper_far()
            diff.append(send(us.at[0, pl.ds(rows_o, 128), :], rs_diff.at[0], ud_s.at[0], ud_r.at[0], cp))
            return
        if not all(v in got for v in UNITS if v[0] == i and v != (3, 3)):
            return
        upper(i)
        rows_same, rows_diff = pl.ds(rows_c, 128), pl.ds(rows_o, 128)
        if i == 3:
            relays.append(send(us.at[3, rows_same, :], relay.at[0], rl_s.at[0], rl_r.at[0], xp(1)))
            relays.append(send(us.at[3, rows_diff, :], relay.at[1], rl_s.at[1], rl_r.at[1], xp(3)))
        elif i == 1:
            diff.append(send(us.at[1, rows_diff, :], rs_diff.at[1], ud_s.at[1], ud_r.at[1], xq(1)))
        elif i == 2:
            same.append(send(us.at[2, rows_same, :], rs_same.at[1], us_s.at[1], us_r.at[1], xp(3)))

    def pass_x(k):
        start = rows_o if k else rows_c
        relays[k].wait_recv()

        def add(t, _):
            r = pl.ds(pl.multiple_of(t * 32, 32), 32)
            at = pl.ds(pl.multiple_of(start + t * 32, 32), 32)
            us[k + 1, at, :] = (uf[k, at, :] + relay[k, r, :].astype(f32)).astype(bf16)
            return 0

        lax.fori_loop(0, 4, add, 0)
        src = us.at[k + 1, pl.ds(start, 128), :]
        if k == 0:
            same.append(send(src, rs_same.at[0], us_s.at[0], us_r.at[0], xp(1)))
        else:
            diff.append(send(src, rs_diff.at[2], ud_s.at[2], ud_r.at[2], xq(3)))

    relays = []
    ready = {0}
    stages = (stage0, relay_y, stage1, stage2, pass_y, stage3)
    owns = (own0, own1, own2, own3, loss0)
    for stage, u in ORDER:
        if stage < 6:
            stages[stage](u)
        elif stage == 6:
            forward_z(u)
        elif stage == 8:
            pass_far(u)
        elif stage == 10:
            pass_x(u)
        else:
            owns[u]()

    mz_wait = hop(mom, mz, zh, mz_r, zp)
    cst.wait_recv()
    ab, s_a, s_b, aa, bb = (own[k : k + 1, :] for k in range(5))
    cii = ab / BATCH
    d = (2.0 * (cii - 1.0)).astype(bf16).astype(f32) - 2.0 * lam * cii
    xme = x * 2 + core
    loss1()
    gathered(mx.at[xme], mz, 4, mz_wait)
    for k in (1, 2, 3):
        send(mx.at[xme], mx.at[xme], None, mx_r.at[0], xp(k))
        send(mx.at[xme], mx.at[xme], None, mx_r.at[0], xq(k))
    send(mx.at[xme], mx.at[xme], None, mx_r.at[0], cp)
    loss2()
    Group(mx.at[0:7], mx_r.at[0]).wait_recv()
    b_sums = mx[0] + mx[2] + mx[4] + mx[6]
    a_sums = mx[1] + mx[3] + mx[5] + mx[7]
    first_b, quad_b, first_a, quad_a = b_sums[0:1], b_sums[1:2], a_sums[0:1], a_sums[1:2]
    one_a = (scale * (first_a + WIDTH * s_a) + d * s_b) / BATCH
    one_b = (scale * (first_b + WIDTH * s_b) + d * s_a) / BATCH
    two_a = (scale * (quad_a + WIDTH * aa) + d * ab) / BATCH
    two_b = (scale * (quad_b + WIDTH * bb) + d * ab) / BATCH
    one_m, two_m = jnp.where(first, one_a, one_b), jnp.where(first, two_a, two_b)
    one_c, two_c = jnp.where(first, one_b, one_a), jnp.where(first, two_b, two_a)
    for c in same + diff:
        c.wait_recv()

    def finish(i, _):
        r = pl.ds(pl.multiple_of(i * 32, 32), 32)
        at = pl.ds(pl.multiple_of(core * 128 + i * 32, 32), 32)
        m, o = nrm[0, at, :].astype(f32), oth[0, at, :].astype(f32)
        up_c = u0[at, :] + rs_same[0, r, :].astype(f32) + rs_same[1, r, :].astype(f32)
        up_m = rs_diff[0, r, :].astype(f32) + rs_diff[1, r, :].astype(f32) + rs_diff[2, r, :].astype(f32)
        up_c = scale * (up_c + WIDTH * o) + d * m
        up_m = scale * (up_m + WIDTH * m) + d * o
        grad_m = up_m - one_m - m * two_m
        grad_c = up_c - one_c - o * two_c
        ga_ref[r, :] = jnp.where(first, grad_m, grad_c)
        gb_ref[r, :] = jnp.where(first, grad_c, grad_m)
        return 0

    lax.fori_loop(0, 4, finish, 0)
    gathered(lsum, lx, 4, pend["loss"])
    loss_ref[...] = lsum[0:1, 0:1]
    rstd_ref[0:1, :] = jnp.where(first, st_mine[1:2, :], st_cross[1:2, :])
    rstd_ref[1:2, :] = jnp.where(first, st_cross[1:2, :], st_mine[1:2, :])
    for c in sends + list(busy.values()):
        c.wait_send()


def local(view_a, view_b):
    dma = pltpu.SemaphoreType.DMA
    vm = pltpu.VMEM
    sems = [
        dma(shape)
        for shape in (
            (2,), (POOL,), (2,), (6,), (4 + 2 * PARTS,), (8,), (2,), (3,), (2,),
            (2,), (6,), (4 + PARTS,), (8,), (2,), (3,), (2,), (NU, 2), (NU,), (NU, 2),
        )
    ] + [dma((1,))] * 11
    vmem = pl.BlockSpec(memory_space=pltpu.VMEM)
    loss, rstd, grad_a, grad_b = pl.pallas_call(
        kernel,
        out_shape=(
            jax.ShapeDtypeStruct((1, 1), f32),
            jax.ShapeDtypeStruct((2, 1024), f32),
            jax.ShapeDtypeStruct((128, 1024), f32),
            jax.ShapeDtypeStruct((128, 1024), f32),
        ),
        in_specs=[pl.BlockSpec(memory_space=pltpu.HBM)] * 2,
        out_specs=(vmem, vmem, vmem, vmem),
        scratch_shapes=[
            vm((128, 1024), bf16), vm((128, 1024), bf16),
            vm((8, 256, 1024), bf16), vm((8, 256, 1024), bf16), vm((8, 256, 1024), bf16),
            vm((128, 1024), bf16),
            vm((4, 2, 1024), f32), vm((4, 2, 1024), f32), vm((8, 1024), f32), vm((8, 1024), f32),
            vm((4, 4, 256, 256), bf16), vm((3, 4, 4, 64, 256), bf16), vm((2, 4, 4, 64, 256), bf16),
            vm((4, 4, 64, 256), bf16), vm((4, 4, 64, 256), bf16),
            vm((4, 4, 256, 256), bf16),
            vm((4, 256, 1024), bf16), vm((256, 1024), f32),
            vm((2, 256, 1024), f32), vm((2, 128, 1024), bf16),
            vm((2, 128, 1024), bf16), vm((3, 128, 1024), bf16),
            vm((2, 1024), f32), vm((8, 2, 1024), f32), vm((4, 2, 1024), f32), vm((NU, 64, 256), bf16),
            vm((8, 1024), f32), vm((4, 8, 1024), f32), vm((4, 8, 1024), f32), vm((2, 8, 1024), f32),
            vm((8, 8, 128), f32), vm((8, 8, 128), f32), vm((4, 8, 128), f32), vm((8, 128), f32),
        ] + sems,
        compiler_params=pltpu.CompilerParams(
            collective_id=0, has_side_effects=True, vmem_limit_bytes=48 * 2**20
        ),
        name="twins",
    )(view_a, view_b)
    return loss[0, 0], rstd[0:1] * grad_a, rstd[1:2] * grad_b


def solution(mesh):
    placed = (P("dp", "feat"), P("dp", "feat"))
    return jax.shard_map(
        local,
        mesh=mesh,
        in_specs=placed,
        out_specs=(P(), P("dp", "feat"), P("dp", "feat")),
        check_vma=False,
    )
```

```python
import jax
import jax.numpy as jnp
from jax import lax
from jax.experimental import pallas as pl
from jax.experimental.pallas import tpu as pltpu
from jax.sharding import PartitionSpec as P

lam = 0.0051
eps = 1e-05
BATCH = 4096.0
WIDTH = 8192.0
MESH = pl.DeviceIdType.MESH
f32 = jnp.float32
bf16 = jnp.bfloat16

OFF = (0, 1, 3, 2)

UNITS = (
    (0, 0), (0, 1), (1, 0), (1, 1), (2, 1), (3, 0), (3, 1), (3, 2),
    (1, 2), (2, 2), (0, 2), (1, 3), (2, 3), (0, 3), (3, 3),
)
NU = len(UNITS)
RING = 11
ORDER = (
    (0, 0), (1, 0), (2, 0), (0, 1), (0, 2), (0, 3), (0, 4), (6, 1), (1, 1), (1, 2),
    (0, 5), (1, 3), (1, 4), (0, 6), (7, 0), (6, 2), (2, 1), (2, 2), (1, 5), (6, 3),
    (2, 3), (2, 4), (1, 6), (8, 0), (3, 0), (0, 7), (6, 4), (7, 1), (2, 5), (8, 1),
    (2, 6), (8, 2), (3, 1), (0, 8), (6, 5), (4, 0), (1, 7), (3, 2), (0, 9), (8, 3),
    (3, 3), (0, 10), (6, 6), (3, 4), (4, 1), (1, 8), (5, 0), (2, 7), (8, 4), (3, 5),
    (4, 2), (1, 9), (6, 7), (3, 6), (4, 3), (1, 10), (4, 4), (8, 5), (5, 1), (2, 8),
    (8, 6), (4, 5), (3, 7), (5, 2), (2, 9), (4, 6), (8, 7), (7, 2), (0, 11), (5, 3),
    (0, 12), (2, 10), (0, 13), (5, 4), (3, 8), (5, 5), (4, 7), (3, 9), (5, 6), (3, 10),
    (2, 11), (0, 14), (2, 12), (2, 13), (4, 8), (5, 7), (3, 11), (4, 9), (4, 10), (3, 12),
    (2, 14), (5, 8), (3, 13), (5, 11), (5, 9), (5, 10), (3, 14), (5, 12), (5, 13), (7, 3),
    (7, 4), (10, 0), (10, 1), (5, 14),
)
POOL = 32
PARTS = 8


def kernel(
    va_hbm, vb_hbm, loss_ref, rstd_ref, ga_ref, gb_ref,
    va, vb, raw, nrm, oth, swap, st_x, st_z, st_mine, st_cross,
    gp, rsy, ps, zs, rz, gf, us, u0, uf, relay, rs_same, rs_diff,
    mom, mx, mz, pc, own, ox, oz, oc2, ly, lz, lx, lsum,
    in_s, pool_s, core_s, gx_s, gz_s, oth_s, us_s, ud_s, rl_s,
    core_r, gx_r, gz_r, oth_r, us_r, ud_r, rl_r, y_r, z_r, ay_r,
    sx_r, sz_r, mx_r, mz_r, pc_r, ox_r, oz_r, o_r, ly_r, lz_r, lx_r,
):
    dp = lax.axis_index("dp")
    ft = lax.axis_index("feat")
    x, zh, core = dp // 8, (dp // 2) % 4, dp % 2
    y, zl = ft // 2, ft % 2

    def dev(ax, az, ac, ay, al):
        return (ax * 8 + az * 2 + ac, ay * 2 + al)

    def xp(d):
        return dev((x + d) % 4, zh, core, y, zl)

    def xq(d):
        return dev((x + d) % 4, zh, 1 - core, y, zl)

    def zp(d):
        return dev(x, (zh + d) % 4, core, y, zl)

    def yp(d):
        return dev(x, zh, core, (y + d) % 4, zl)

    def zq(d):
        return dev(x, (zh + d) % 4, 1 - core, y, zl)

    def yq(d):
        return dev(x, zh, core, (y + d) % 4, 1 - zl)

    cp = dev(x, zh, 1 - core, y, zl)
    lp = dev(x, zh, core, y, 1 - zl)

    sends, busy, turn = [], {}, [0]

    def send(src, dst, ss, rs, to):
        slot = None
        if ss is None:
            slot = turn[0] % POOL
            turn[0] += 1
            if slot in busy:
                busy[slot].wait_send()
            ss = pool_s.at[slot]
        c = pltpu.make_async_remote_copy(
            src_ref=src, dst_ref=dst, send_sem=ss, recv_sem=rs, device_id=to, device_id_type=MESH
        )
        c.start()
        if slot is None:
            sends.append(c)
        else:
            busy[slot] = c
        return c

    class Group:
        def __init__(self, buf, rs):
            self.buf, self.rs = buf, rs

        def wait_recv(self):
            pltpu.make_async_remote_copy(
                src_ref=self.buf, dst_ref=self.buf, send_sem=pool_s.at[0], recv_sem=self.rs,
                device_id=cp, device_id_type=MESH,
            ).wait_recv()

    loads = [
        pltpu.make_async_copy(src, dst, in_s.at[k])
        for k, (src, dst) in enumerate(((va_hbm, va), (vb_hbm, vb)))
    ]
    for c in loads:
        c.start()
    barrier = pltpu.get_barrier_semaphore()
    peers = [cp, lp]
    for d in (1, 2, 3):
        peers += [xp(d), xq(d), zp(d), zq(d), yp(d), yq(d)]
    for p in peers:
        pl.semaphore_signal(barrier, inc=1, device_id=p, device_id_type=MESH)

    first = core == 0
    rows_c = pl.multiple_of(core * 128, 128)
    rows_o = pl.multiple_of((1 - core) * 128, 128)

    for c in loads:
        c.wait()

    def split(i, _):
        r = pl.ds(pl.multiple_of(i * 32, 32), 32)
        a, b = va[r, :], vb[r, :]
        raw[0, pl.ds(pl.multiple_of(core * 128 + i * 32, 32), 32), :] = jnp.where(first, a, b)
        swap[r, :] = jnp.where(first, b, a)
        return 0

    lax.fori_loop(0, 4, split, 0)
    pl.semaphore_wait(barrier, len(peers))

    c = send(swap, raw.at[0, pl.ds(rows_c, 128), :], core_s.at[0], core_r.at[0], cp)
    c.wait_recv()

    lo, hi = pl.ds(0, 128), pl.ds(128, 128)
    own_lo, own_hi = raw.at[0, lo, :], raw.at[0, hi, :]

    def ring(next_lo, next_hi, prev_lo, prev_hi, ss, rs, to):
        return (
            send(own_lo, prev_lo, ss.at[0], rs.at[0], to(1)),
            send(own_hi, next_hi, ss.at[1], rs.at[1], to(3)),
            send(own_hi, prev_hi, ss.at[2], rs.at[2], to(1)),
            send(own_lo, next_lo, ss.at[3], rs.at[3], to(3)),
        )

    def forward(prev_lo, next_hi, far, ss, rs, to, near):
        near[0].wait_recv()
        send(prev_lo, raw.at[far, lo, :], ss.at[4], rs.at[4], to(1))
        near[1].wait_recv()
        send(next_hi, raw.at[far, hi, :], ss.at[5], rs.at[4], to(3))
        return [Group(raw.at[far], rs.at[4])]

    def sums(i, acc):
        v = raw[0, pl.ds(pl.multiple_of(i * 32, 32), 32), :].astype(f32)
        return acc + jnp.sum(v.reshape(4, 8, 1024), axis=0)

    mean = jnp.sum(lax.fori_loop(0, 8, sums, jnp.zeros((8, 1024), f32)), axis=0, keepdims=True) / 256.0

    def squares(i, acc):
        v = raw[0, pl.ds(pl.multiple_of(i * 32, 32), 32), :].astype(f32) - mean
        return acc + jnp.sum((v * v).reshape(4, 8, 1024), axis=0)

    m2 = jnp.sum(lax.fori_loop(0, 8, squares, jnp.zeros((8, 1024), f32)), axis=0, keepdims=True)

    def combine(buf, count):
        means = [buf[k, 0:1, :] for k in range(4)]
        avg = (means[0] + means[1] + means[2] + means[3]) * 0.25
        total = buf[0, 1:2, :] + buf[1, 1:2, :] + buf[2, 1:2, :] + buf[3, 1:2, :]
        dev2 = sum((m - avg) * (m - avg) for m in means)
        return avg, total + count * dev2

    def spread(value_a, value_b, buf, me, rs, to):
        buf[me, 0:1, :] = value_a
        buf[me, 1:2, :] = value_b
        for d in (1, 2, 3):
            send(buf.at[me], buf.at[me], None, rs.at[0], to(d))
        return [Group(buf.at[0:3], rs.at[0])]

    sz = spread(mean, m2, st_z, zh, sz_r, zp)
    gz = ring(
        raw.at[5, lo, :], raw.at[4, lo, :], raw.at[4, hi, :], raw.at[5, hi, :], gz_s, gz_r, zp
    )
    for c in sz:
        c.wait_recv()
    mean, m2 = combine(st_z, 256.0)
    sx = spread(mean, m2, st_x, x, sx_r, xp)
    gx = ring(
        raw.at[1, lo, :], raw.at[1, hi, :], raw.at[2, lo, :], raw.at[2, hi, :], gx_s, gx_r, xp
    )
    for c in sx:
        c.wait_recv()
    mean, m2 = combine(st_x, 1024.0)
    rstd = lax.rsqrt(m2 / BATCH + eps)
    st_mine[0:1, :] = mean
    st_mine[1:2, :] = rstd
    cst = send(st_mine, st_cross, core_s.at[1], core_r.at[1], cp)

    def normalize(k):
        def step(i, _):
            r = pl.ds(pl.multiple_of(i * 32, 32), 32)
            v = raw[k, r, :].astype(f32)
            nrm[k, r, :] = ((v - st_mine[0:1, :]) * st_mine[1:2, :]).astype(bf16)
            return 0

        lax.fori_loop(0, 8, step, 0)
        return send(nrm.at[k], oth.at[k], oth_s.at[k], oth_r.at[k], cp)

    oc = {0: normalize(0)}
    far = {}

    def forward_x():
        far["x"] = forward(raw.at[2, lo, :], raw.at[1, hi, :], 3, gx_s, gx_r, xp, gx)

    passed = {}

    def forward_z(k):
        if k >= PARTS:
            return
        n = 128 // PARTS
        for e, (half, to) in enumerate(((1, 1), (0, 3))):
            if k == 0:
                gz[e].wait_recv()
            src = raw.at[4, pl.ds(half * 128 + k * n, n), :]
            dst = raw.at[6, pl.ds((1 - half) * 128 + k * n, n), :]
            at = 4 + (2 * k + e) % 8
            if at in passed:
                passed[at].wait_send()
                sends[:] = [c for c in sends if c is not passed[at]]
            passed[at] = send(src, dst, gz_s.at[at], gz_r.at[4 + k], zp(to))

    def pass_far(k):
        n = 128 // PARTS
        Group(raw.at[6, pl.ds(0, 2 * n), :], gz_r.at[4 + k]).wait_recv()
        for half in range(2):
            rows = pl.ds(half * 128 + k * n, n)
            send(raw.at[6, rows, :], raw.at[7, rows, :], None, gx_r.at[5], xp(2))

    arrive = {
        1: lambda: gx[3].wait_recv(),
        2: lambda: gx[2].wait_recv(),
        3: lambda: [c.wait_recv() for c in far["x"]],
        4: lambda: [forward_x(), forward_z(0)],
        5: lambda: [gz[2].wait_recv(), gz[3].wait_recv()],
        6: lambda: None,
        7: lambda: Group(raw.at[7], gx_r.at[5]).wait_recv(),
    }

    def need(k):
        if k not in oc:
            arrive[k]()
            oc[k] = normalize(k)

    piece = pl.multiple_of(y * 64, 64)
    nt = (((1,), (1,)), ((), ()))
    eye = (
        lax.broadcasted_iota(jnp.int32, (256, 256), 0) == lax.broadcasted_iota(jnp.int32, (256, 256), 1)
    )

    ry, zx, ay = {}, {}, {}
    mine = pl.ds(piece, 64)

    def rows_of(d, at=0, n=64):
        return pl.ds(pl.multiple_of(((y + d) % 4) * 64 + at, 32), n)

    def blocks_of(u):
        i, j = UNITS[u]
        return (0, 7) if (i, j) == (3, 3) else (i, 3 + j if j else 0)

    def stage0(u):
        i, j = UNITS[u]
        row, col = blocks_of(u)
        need(col)
        need(row)
        g = lax.dot_general(nrm[row], nrm[col], nt, preferred_element_type=f32)
        if i == 0 and j == 0:
            g = jnp.where(eye, g - WIDTH / 8, g)
        gp[i, j] = g.astype(bf16)
        if u < RING:
            for half, to in ((0, 1), (1, 3)):
                src = gp.at[i, j, rows_of(2, half * 32, 32), :]
                send(src, rsy.at[2, i, j, pl.ds(half * 32, 32), :], None, y_r.at[u, 0], yp(to))
            ry[u] = Group(rsy.at[2, i, j], y_r.at[u, 0])
        else:
            for d in (2, 1, 3):
                send(gp.at[i, j, rows_of(d), :], rsy.at[d - 1, i, j], None, y_r.at[u, 1], yp(d))
            ry[u] = Group(rsy.at[:, i, j], y_r.at[u, 1])

    def relay_y(u):
        i, j = UNITS[u]
        ry[u].wait_recv()
        up = rsy[2, i, j, 0:32, :].astype(f32) + gp[i, j, rows_of(1, 0, 32), :].astype(f32)
        ps[0, i, j, 0:32, :] = up.astype(bf16)
        ps[0, i, j, 32:64, :] = gp[i, j, rows_of(1, 32, 32), :]
        down = rsy[2, i, j, 32:64, :].astype(f32) + gp[i, j, rows_of(3, 32, 32), :].astype(f32)
        ps[1, i, j, 0:32, :] = gp[i, j, rows_of(3, 0, 32), :]
        ps[1, i, j, 32:64, :] = down.astype(bf16)
        for k in range(2):
            send(ps.at[k, i, j], rsy.at[k, i, j], None, y_r.at[u, 1], yp(1 + 2 * k))
        ry[u] = Group(rsy.at[0:2, i, j], y_r.at[u, 1])

    def stage1(u):
        i, j = UNITS[u]
        ry[u].wait_recv()
        total = gp[i, j, mine, :].astype(f32)
        for k in range(2 if u < RING else 3):
            total = total + rsy[k, i, j].astype(f32)
        zs[i, j] = total.astype(bf16)
        zx[u] = send(zs.at[i, j], rz.at[i, j], None, z_r.at[u], lp)

    def stage2(u):
        i, j = UNITS[u]
        zx[u].wait_recv()
        gf[i, j, mine, :] = (zs[i, j].astype(f32) + rz[i, j].astype(f32)).astype(bf16)
        at = gf.at[i, j, mine, :]
        send(at, pc.at[u], None, pc_r.at[0], cp)
        for d in (1, 3) if u < RING else (2, 1, 3):
            send(at, at, None, ay_r.at[u, 0], yp(d))
        ay[u] = Group(rsy.at[0:2, i, j] if u < RING else rsy.at[:, i, j], ay_r.at[u, 0])

    def pass_y(u):
        i, j = UNITS[u]
        ay[u].wait_recv()
        a = gf.at[i, j, rows_of(3, 0, 32), :]
        b = gf.at[i, j, rows_of(1, 32, 32), :]
        send(a, a, None, ay_r.at[u, 1], yp(1))
        send(b, b, None, ay_r.at[u, 1], yp(3))
        ay[u] = Group(rsy.at[2, i, j], ay_r.at[u, 1])

    def step_own(i, acc):
        at = pl.ds(pl.multiple_of(core * 128 + i * 32, 32), 32)
        m, o = nrm[0, at, :].astype(f32), oth[0, at, :].astype(f32)
        return tuple(
            q + jnp.sum(v.reshape(4, 8, 1024), axis=0) for q, v in zip(acc, (m * o, m, o, m * m, o * o))
        )

    def hop(src, buf, me, rs, to):
        buf[me] = src[...]
        for d in (1, 2, 3):
            send(buf.at[me], buf.at[me], None, rs.at[0], to(d))
        return [Group(buf.at[0:3], rs.at[0])]

    def swap_cores(src, buf, rs):
        buf[core] = src[...]
        return [send(buf.at[core], buf.at[core], None, rs.at[0], cp)]

    def gathered(dst, buf, n, cs):
        for c in cs:
            c.wait_recv()
        total = buf[0]
        for k in range(1, n):
            total = total + buf[k]
        dst[...] = total

    pend = {}

    def own0():
        oc[0].wait_recv()
        ab, sm, so, mm, oo = (
            jnp.sum(v, axis=0, keepdims=True)
            for v in lax.fori_loop(0, 4, step_own, (jnp.zeros((8, 1024), f32),) * 5)
        )
        rows = (
            ab, jnp.where(first, sm, so), jnp.where(first, so, sm),
            jnp.where(first, mm, oo), jnp.where(first, oo, mm),
        )
        for k, v in enumerate(rows):
            own[k : k + 1, :] = v
        own[5:8, :] = jnp.zeros((3, 1024), f32)
        pend["own"] = hop(own, ox, x, ox_r, xp)

    def own1():
        gathered(own, ox, 4, pend["own"])
        pend["own"] = swap_cores(own, oc2, o_r)

    def own2():
        gathered(own, oc2, 2, pend["own"])
        pend["own"] = hop(own, oz, zh, oz_r, zp)

    def own3():
        gathered(own, oz, 4, pend["own"])

    scale = 2.0 * lam / BATCH

    def loss0():
        Group(pc, pc_r.at[0]).wait_recv()
        acc = jnp.zeros((8, 256), f32)
        for u, (i, j) in enumerate(UNITS):
            g, h = gf[i, j, mine, :].astype(f32), pc[u].astype(f32)
            if i == 0 and j == 0:
                here = lax.broadcasted_iota(jnp.int32, (64, 256), 0) + piece
                here = here == lax.broadcasted_iota(jnp.int32, (64, 256), 1)
                g, h = jnp.where(here, g + WIDTH, g), jnp.where(here, h + WIDTH, h)
            p = jnp.sum((g * h).reshape(8, 8, 256), axis=0)
            acc = acc + (2.0 * p if (i, j) == (1, 0) else p)
        pairs = jnp.sum(jnp.sum(acc, axis=0, keepdims=True), axis=1, keepdims=True) / (BATCH * BATCH)
        cii = own[0:1, :] / BATCH
        terms = jnp.sum((1.0 - cii) * (1.0 - cii) - lam * cii * cii, axis=1, keepdims=True)
        ly[ft] = jnp.broadcast_to(0.25 * lam * pairs + terms / 32.0, (8, 128))
        for k in (1, 2, 3):
            send(ly.at[ft], ly.at[ft], None, ly_r.at[0], yp(k))
            send(ly.at[ft], ly.at[ft], None, ly_r.at[0], yq(k))
        send(ly.at[ft], ly.at[ft], None, ly_r.at[0], lp)

    def loss1():
        lme = zh * 2 + core
        gathered(lz.at[lme], ly, 8, [Group(ly.at[0:7], ly_r.at[0])])
        for k in (1, 2, 3):
            send(lz.at[lme], lz.at[lme], None, lz_r.at[0], zp(k))
            send(lz.at[lme], lz.at[lme], None, lz_r.at[0], zq(k))
        send(lz.at[lme], lz.at[lme], None, lz_r.at[0], cp)

    def loss2():
        gathered(lsum, lz, 8, [Group(lz.at[0:7], lz_r.at[0])])
        pend["loss"] = hop(lsum, lx, x, lx_r, xp)

    mom[...] = jnp.zeros((2, 1024), f32)
    tn = (((0,), (0,)), ((), ()))
    nn = (((1,), (0,)), ((), ()))

    def product(i, terms, store, after=None):
        def tile(t, _):
            cols = pl.ds(t * 256 if after is not None else pl.multiple_of(t * 256, 256), 256)
            acc = jnp.zeros((256, 256), f32)
            for p, q, k, how in terms:
                acc = acc + lax.dot_general(gf[p, q], oth[k, :, cols], how, preferred_element_type=f32)
            mom[0:1, cols] += jnp.sum(acc, axis=0, keepdims=True)
            mom[1:2, cols] += jnp.sum(acc * oth[i, :, cols].astype(f32), axis=0, keepdims=True)
            store(cols, acc)
            if after is not None:
                after(cols)
            return 0

        if after is None:
            lax.fori_loop(0, 4, tile, 0)
        else:
            for t in range(4):
                tile(t, 0)

    def upper(i):
        terms = [(i, j, 3 + j if j else 0, nn) for j in range(4) if (i, j) in UNITS and (i, j) != (3, 3)]

        def store(cols, acc):
            if i == 0:
                u0[:, cols] = acc
            else:
                us[i, :, cols] = acc.astype(bf16)
            if i in (1, 2):
                uf[i - 1, :, cols] = acc

        def leave(cols):
            if i == 1:
                send(us.at[1, pl.ds(rows_o, 128), cols], rs_diff.at[1, :, cols], None, ud_r.at[1], xq(1))
            else:
                send(us.at[2, pl.ds(rows_c, 128), cols], rs_same.at[1, :, cols], None, us_r.at[1], xp(3))

        if i == 0:
            terms = terms + [(1, 0, 1, tn)]
        product(i, terms, store, leave if i in (1, 2) else None)

    def upper_far():
        def store(cols, acc):
            acc = acc + u0[:, cols]
            u0[:, cols] = acc
            us[0, :, cols] = acc.astype(bf16)

        product(0, [(3, 3, 7, nn)], store)

    same, diff = [], []
    got = set()

    def stage3(u):
        ay[u].wait_recv()
        got.add(UNITS[u])
        i, j = UNITS[u]
        for k in blocks_of(u) + (1,):
            if k not in ready and k in oc:
                ready.add(k)
                oc[k].wait_recv()
        if (i, j) == (3, 3):
            upper_far()
            diff.append(send(us.at[0, pl.ds(rows_o, 128), :], rs_diff.at[0], ud_s.at[0], ud_r.at[0], cp))
            return
        if not all(v in got for v in UNITS if v[0] == i and v != (3, 3)):
            return
        upper(i)
        rows_same, rows_diff = pl.ds(rows_c, 128), pl.ds(rows_o, 128)
        if i == 3:
            relays.append(send(us.at[3, rows_same, :], relay.at[0], rl_s.at[0], rl_r.at[0], xp(1)))
            relays.append(send(us.at[3, rows_diff, :], relay.at[1], rl_s.at[1], rl_r.at[1], xp(3)))
        elif i == 1:
            diff.append(Group(rs_diff.at[1], ud_r.at[1]))
        elif i == 2:
            same.append(Group(rs_same.at[1], us_r.at[1]))

    def pass_x(k):
        start = rows_o if k else rows_c
        relays[k].wait_recv()

        def add(t, _):
            r = pl.ds(pl.multiple_of(t * 32, 32), 32)
            at = pl.ds(pl.multiple_of(start + t * 32, 32), 32)
            us[k + 1, at, :] = (uf[k, at, :] + relay[k, r, :].astype(f32)).astype(bf16)
            return 0

        lax.fori_loop(0, 4, add, 0)
        src = us.at[k + 1, pl.ds(start, 128), :]
        if k == 0:
            same.append(send(src, rs_same.at[0], us_s.at[0], us_r.at[0], xp(1)))
        else:
            diff.append(send(src, rs_diff.at[2], ud_s.at[2], ud_r.at[2], xq(3)))

    relays = []
    ready = {0}
    stages = (stage0, relay_y, stage1, stage2, pass_y, stage3)
    owns = (own0, own1, own2, own3, loss0)
    for stage, u in ORDER:
        if stage < 6:
            stages[stage](u)
        elif stage == 6:
            forward_z(u)
        elif stage == 8:
            pass_far(u)
        elif stage == 10:
            pass_x(u)
        else:
            owns[u]()

    mz_wait = hop(mom, mz, zh, mz_r, zp)
    cst.wait_recv()
    ab, s_a, s_b, aa, bb = (own[k : k + 1, :] for k in range(5))
    cii = ab / BATCH
    d = (2.0 * (cii - 1.0)).astype(bf16).astype(f32) - 2.0 * lam * cii
    xme = x * 2 + core
    loss1()
    gathered(mx.at[xme], mz, 4, mz_wait)
    for k in (1, 2, 3):
        send(mx.at[xme], mx.at[xme], None, mx_r.at[0], xp(k))
        send(mx.at[xme], mx.at[xme], None, mx_r.at[0], xq(k))
    send(mx.at[xme], mx.at[xme], None, mx_r.at[0], cp)
    loss2()
    Group(mx.at[0:7], mx_r.at[0]).wait_recv()
    b_sums = mx[0] + mx[2] + mx[4] + mx[6]
    a_sums = mx[1] + mx[3] + mx[5] + mx[7]
    first_b, quad_b, first_a, quad_a = b_sums[0:1], b_sums[1:2], a_sums[0:1], a_sums[1:2]
    one_a = (scale * (first_a + WIDTH * s_a) + d * s_b) / BATCH
    one_b = (scale * (first_b + WIDTH * s_b) + d * s_a) / BATCH
    two_a = (scale * (quad_a + WIDTH * aa) + d * ab) / BATCH
    two_b = (scale * (quad_b + WIDTH * bb) + d * ab) / BATCH
    one_m, two_m = jnp.where(first, one_a, one_b), jnp.where(first, two_a, two_b)
    one_c, two_c = jnp.where(first, one_b, one_a), jnp.where(first, two_b, two_a)
    for c in same + diff:
        c.wait_recv()

    def finish(i, _):
        r = pl.ds(pl.multiple_of(i * 32, 32), 32)
        at = pl.ds(pl.multiple_of(core * 128 + i * 32, 32), 32)
        m, o = nrm[0, at, :].astype(f32), oth[0, at, :].astype(f32)
        up_c = u0[at, :] + rs_same[0, r, :].astype(f32) + rs_same[1, r, :].astype(f32)
        up_m = rs_diff[0, r, :].astype(f32) + rs_diff[1, r, :].astype(f32) + rs_diff[2, r, :].astype(f32)
        up_c = scale * (up_c + WIDTH * o) + d * m
        up_m = scale * (up_m + WIDTH * m) + d * o
        grad_m = up_m - one_m - m * two_m
        grad_c = up_c - one_c - o * two_c
        ga_ref[r, :] = jnp.where(first, grad_m, grad_c)
        gb_ref[r, :] = jnp.where(first, grad_c, grad_m)
        return 0

    lax.fori_loop(0, 4, finish, 0)
    gathered(lsum, lx, 4, pend["loss"])
    loss_ref[...] = lsum[0:1, 0:1]
    rstd_ref[0:1, :] = jnp.where(first, st_mine[1:2, :], st_cross[1:2, :])
    rstd_ref[1:2, :] = jnp.where(first, st_cross[1:2, :], st_mine[1:2, :])
    for c in sends + list(busy.values()):
        c.wait_send()


def local(view_a, view_b):
    dma = pltpu.SemaphoreType.DMA
    vm = pltpu.VMEM
    sems = [
        dma(shape)
        for shape in (
            (2,), (POOL,), (2,), (6,), (12,), (8,), (2,), (3,), (2,),
            (2,), (6,), (4 + PARTS,), (8,), (2,), (3,), (2,), (NU, 2), (NU,), (NU, 2),
        )
    ] + [dma((1,))] * 11
    vmem = pl.BlockSpec(memory_space=pltpu.VMEM)
    loss, rstd, grad_a, grad_b = pl.pallas_call(
        kernel,
        out_shape=(
            jax.ShapeDtypeStruct((1, 1), f32),
            jax.ShapeDtypeStruct((2, 1024), f32),
            jax.ShapeDtypeStruct((128, 1024), f32),
            jax.ShapeDtypeStruct((128, 1024), f32),
        ),
        in_specs=[pl.BlockSpec(memory_space=pltpu.HBM)] * 2,
        out_specs=(vmem, vmem, vmem, vmem),
        scratch_shapes=[
            vm((128, 1024), bf16), vm((128, 1024), bf16),
            vm((8, 256, 1024), bf16), vm((8, 256, 1024), bf16), vm((8, 256, 1024), bf16),
            vm((128, 1024), bf16),
            vm((4, 2, 1024), f32), vm((4, 2, 1024), f32), vm((8, 1024), f32), vm((8, 1024), f32),
            vm((4, 4, 256, 256), bf16), vm((3, 4, 4, 64, 256), bf16), vm((2, 4, 4, 64, 256), bf16),
            vm((4, 4, 64, 256), bf16), vm((4, 4, 64, 256), bf16),
            vm((4, 4, 256, 256), bf16),
            vm((4, 256, 1024), bf16), vm((256, 1024), f32),
            vm((2, 256, 1024), f32), vm((2, 128, 1024), bf16),
            vm((2, 128, 1024), bf16), vm((3, 128, 1024), bf16),
            vm((2, 1024), f32), vm((8, 2, 1024), f32), vm((4, 2, 1024), f32), vm((NU, 64, 256), bf16),
            vm((8, 1024), f32), vm((4, 8, 1024), f32), vm((4, 8, 1024), f32), vm((2, 8, 1024), f32),
            vm((8, 8, 128), f32), vm((8, 8, 128), f32), vm((4, 8, 128), f32), vm((8, 128), f32),
        ] + sems,
        compiler_params=pltpu.CompilerParams(
            collective_id=0, has_side_effects=True, vmem_limit_bytes=48 * 2**20
        ),
        name="twins",
    )(view_a, view_b)
    return loss[0, 0], rstd[0:1] * grad_a, rstd[1:2] * grad_b


def solution(mesh):
    placed = (P("dp", "feat"), P("dp", "feat"))
    return jax.shard_map(
        local,
        mesh=mesh,
        in_specs=placed,
        out_specs=(P(), P("dp", "feat"), P("dp", "feat")),
        check_vma=False,
    )
```
